128 devices in a mesh: grp: 8 (over y, core), tp: 16 (over z, x).
Axes of the slice: x: 4, y: 4, z: 4, core: 2. Of those that a mesh axis runs over, the one named last changes fastest.
Arguments:
- queries: bfloat16 [1024, 4096], P('grp', 'tp'), may hold values from -6 to 6
- new_kv: bfloat16 [1024, 16, 256], P('grp', 'tp'), may hold values from -6 to 6, as said below
- kv_cache: bfloat16 [3200, 16, 16, 256], P('grp', 'tp'), may hold values from -6 to 6, as said below
- page_table: int32 [1024, 16], P('grp'), may hold values from 0 to 399, as said below
- context_lengths: int32 [1024], P('grp'), may hold values from 1 to 256, as said below
- out_weight: bfloat16 [4096, 6144], P('tp'), may hold values from -0.09375 to 0.09375
- residual_in: bfloat16 [1024, 6144], P('grp', 'tp'), may hold values from -32 to 32
- norm_gain: float32 [6144], replicated, may hold values from 0.5 to 1.5
- router_weight: bfloat16 [6144, 8], replicated, may hold values from -0.078125 to 0.078125
- routes: int32 [1024, 2], P('grp'), may hold values from 0 to 7, all different within a row; in each aligned block of 128 rows (0 to 127, 128 to 255, ...) at most 64 rows name the same one
- gate_weight: bfloat16 [8, 6144, 8192], P('grp', None, 'tp'), may hold values from -0.078125 to 0.078125
- up_weight: bfloat16 [8, 6144, 8192], P('grp', None, 'tp'), may hold values from -0.078125 to 0.078125
- down_weight: bfloat16 [8, 8192, 6144], P('grp', 'tp'), may hold values from -0.0625 to 0.0625
Outputs:
- layer_out: bfloat16 [1024, 6144], P('grp', 'tp')
The draws below stay inside these ranges and needn't reach their ends.
Inputs may be any that keep to these rules, and one draw needn't show every extreme that they name: `context_lengths`: cached tokens of each request, its new token not counted. In every group of 128 requests one has exactly 256, and the pages they need, ceil(length / 16) each, sum to at most 400. `page_table`: entries index the pool of the request's own group. The first ceil(length / 16) entries of all requests of one group are distinct; later entries name arbitrary pages. `routes`: two different experts for each token. Among the 128 tokens of one group at most 64 name the same expert, a bound that some group reaches. `kv_cache`: copy c holds key-value head c * 8 // 16; copies of one head are equal. `new_kv`: copy c holds key-value head c * 8 // 16; copies of one head are equal.
All inputs are finite; a program needn't handle non-finite values.
Results may differ from the reference program's by a relative error of at most 0.011.
Values may be sent and summed in bfloat16 or wider, within the bound.
A program may use at most 128 MiB of HBM per device.

```python
import math
import jax
import jax.numpy as jnp
import numpy as np
from jax import lax

D = 6144
FF = 8192
H = 32
KVH = 8
HD = 128
PAGE = 16
LMAX = 256
REQ = 128
E = 8
TOKENS = 1024
CAP = 64
PPR = 16
EXTRA = 256
POOL = 400
N_GRP = 8
N_TP = 16


def layout_draw(key):
    key_list = jax.random.split(key, 6)
    group_count = N_GRP
    draw_first = jax.random.randint(key_list[0], (group_count, EXTRA), 0, REQ)
    draw_second = jax.random.randint(key_list[1], (group_count, EXTRA), 0, REQ)
    page_owner = jnp.minimum(draw_first, draw_second)
    slot_ids = jnp.arange(REQ, dtype=jnp.int32)
    counts = jnp.sum((page_owner[:, :, None] == slot_ids[None, None, :]).astype(jnp.int32), axis=1)
    page_need = 1 + jnp.minimum(counts, PPR - 1)
    within = jax.random.randint(key_list[2], (group_count, REQ), 1, PAGE + 1)
    lengths = (page_need - 1) * PAGE + within
    forced = jax.random.randint(key_list[3], (group_count, 1), 0, REQ)
    chosen = slot_ids[None, :] == forced
    page_need = jnp.where(chosen, PPR, page_need)
    lengths = jnp.where(chosen, LMAX, lengths)

    def shuffle_requests(sub_key):
        return jax.random.permutation(sub_key, REQ)

    def shuffle_pool(sub_key):
        return jax.random.permutation(sub_key, POOL)
    req_order = jax.vmap(shuffle_requests)(jax.random.split(key_list[4], group_count))
    page_need = jnp.take_along_axis(page_need, req_order, axis=1)
    lengths = jnp.take_along_axis(lengths, req_order, axis=1)
    starts = jnp.cumsum(page_need, axis=1) - page_need
    places = jax.vmap(shuffle_pool)(jax.random.split(key_list[5], group_count))
    offsets = (starts[:, :, None] + jnp.arange(PPR, dtype=jnp.int32)[None, None, :]) % POOL
    page_map = jnp.take_along_axis(places, offsets.reshape(group_count, REQ * PPR), axis=1)
    return (lengths.reshape(TOKENS).astype(jnp.int32), page_map.reshape(TOKENS, PPR).astype(jnp.int32))


def draw_context_lengths(key, part):
    lengths, page_map = layout_draw(key)
    return lengths


def draw_page_table(key, part):
    lengths, page_map = layout_draw(key)
    return page_map


def draw_queries(key, part):
    key = jax.random.fold_in(key, 1)
    base_vals = jnp.clip(jax.random.normal(key, (TOKENS, H, HD), jnp.float32), -6.0, 6.0)
    return base_vals.reshape(TOKENS, H * HD).astype(jnp.bfloat16)


def draw_new_kv(key, part):
    key = jax.random.fold_in(key, 2)
    base_vals = jnp.clip(jax.random.normal(key, (TOKENS, KVH, 2 * HD), jnp.float32), -6.0, 6.0)
    return jnp.repeat(base_vals, N_TP // KVH, axis=1).astype(jnp.bfloat16)


def draw_kv_cache(key, part):
    key = jax.random.fold_in(key, 3)
    shape_all = (N_GRP * POOL, KVH, PAGE, 2 * HD)
    base_vals = jnp.clip(jax.random.normal(key, shape_all, jnp.float32), -6.0, 6.0)
    return jnp.repeat(base_vals, N_TP // KVH, axis=1).astype(jnp.bfloat16)


def draw_residual_in(key, part):
    key = jax.random.fold_in(key, 4)
    sub_first = jax.random.fold_in(key, 0)
    col_pos = jnp.arange(D, dtype=jnp.float32) / D
    base_vals = jnp.clip(jax.random.normal(sub_first, (TOKENS, D), jnp.float32), -6.0, 6.0)
    base_vals = base_vals * jnp.exp(col_pos * 1.0986)[None, :]
    return base_vals.astype(jnp.bfloat16)


def block_scale(own_key, extent, cuts, least, largest):
    level, own = 1.0, jax.random.fold_in(own_key, 6)
    for position, parts in cuts:
        heights = jnp.exp(jax.random.uniform(jax.random.fold_in(own, position), (parts,), jnp.float32, least / len(cuts), largest / len(cuts)))
        level = level * jnp.repeat(heights, extent[position] // parts).reshape([-1 if axis == position else 1 for axis in range(len(extent))])
    return level


def deal_out(key, own, number, rows, amount, top, bound, slope):
    sequence = jax.random.permutation(key, amount)
    crowded, ordinary = shares(amount, rows * top, bound, slope, True), shares(amount, rows * top, bound, slope, False)
    places = jnp.arange(amount)

    def named(sizes, turn):
        used = int((sizes > 0).sum())
        fixed = max(1, used // 4)
        shifted = fixed + (places - fixed + turn * (used - fixed)) % max(1, amount - fixed)
        return jnp.zeros((amount,), jnp.int32).at[sequence[jnp.where(places < fixed, places, shifted)]].set(jnp.asarray(sizes, jnp.int32))

    sizes = jnp.where(number % 4 == 0, named(crowded, number // 4), named(ordinary, number - number // 4 - 1))
    mixed = jax.random.permutation(jax.random.fold_in(own, 3), amount)
    source_of, taker = mixed[0:amount // 2 * 2:2], mixed[1:amount // 2 * 2:2]
    room = jnp.minimum(sizes[source_of] - 1, bound - sizes[taker]) // 2
    room = jnp.where((source_of == sequence[0]) | (taker == sequence[0]) | (sizes[taker] == 0), 0, jnp.maximum(room, 0))
    shifted = jax.random.randint(jax.random.fold_in(own, 4), (amount // 2,), 0, 1 << 20) % (room + 1)
    sizes = sizes.at[source_of].add(-shifted).at[taker].add(shifted)
    items = jnp.searchsorted(jnp.cumsum(sizes), jnp.arange(rows * top), side="right").astype(jnp.int32)
    table = items.reshape(top, rows).T
    table = table[jax.random.permutation(jax.random.fold_in(own, 1), rows)]
    turn = jax.random.randint(jax.random.fold_in(own, 2), (rows, 1), 0, top)
    return jnp.take_along_axis(table, (jnp.arange(top)[None, :] + turn) % top, axis=1)


def shares(number_of, total, limit, lean, full):
    portions = [(1 << 20) // math.isqrt(rank ** lean) + 1 for rank in range(1, number_of + 1)]
    largest = limit if full else min(limit, max(-(-total // number_of), total * portions[0] // sum(portions)))
    least = 1 if total - largest >= number_of - 1 else 0
    holding, surplus = [largest] + [least] * (number_of - 1), total - largest - least * (number_of - 1)
    while surplus > 0:
        free = [i for i in range(1, number_of) if holding[i] < largest] or [i for i in range(1, number_of) if holding[i] < limit]
        whole, budget = sum([portions[i] for i in free]), surplus
        for i in free:
            addition = min(limit - holding[i], max(1, budget * portions[i] // whole), surplus)
            holding[i] = holding[i] + addition
            surplus = surplus - addition
    return np.array(holding)


def gaussian(rng, shape, spread, bound, pieces=(), kind=jnp.bfloat16):
    level = block_scale(rng, shape, pieces, -0.22, 0.18) if pieces else 1.0
    entries = jax.random.normal(rng, shape, jnp.float32) * spread * level
    return jnp.minimum(jnp.maximum(entries, -bound), bound).astype(kind)


def setup_inputs(seed: int = 0) -> dict:
    keys = jax.random.split(jax.random.key(seed), 14)
    queries = draw_queries(jax.random.fold_in(keys[13], 71), 0)
    new_kv = draw_new_kv(jax.random.fold_in(keys[13], 71), 0)
    kv_cache = draw_kv_cache(jax.random.fold_in(keys[13], 71), 0)
    page_table = draw_page_table(jax.random.fold_in(keys[13], 71), 0)
    context_lengths = draw_context_lengths(jax.random.fold_in(keys[13], 71), 0)
    out_weight = gaussian(keys[5], (H * HD, D), (H * HD) ** -0.5, 0.09375, ((0, 16),))
    residual_in = draw_residual_in(jax.random.fold_in(keys[13], 71), 0)
    norm_gain = jnp.clip(1.0 + 0.1 * jax.random.normal(keys[7], (D,), jnp.float32), 0.5, 1.5)
    router_weight = gaussian(keys[8], (D, E), D ** -0.5, 0.078125)
    routes_keys = jax.random.split(jax.random.fold_in(keys[9], 1), TOKENS // REQ)
    routes_turns = jax.random.permutation(jax.random.fold_in(keys[9], 3), TOKENS // REQ)
    routes = jax.vmap(lambda own, number: deal_out(jax.random.fold_in(keys[9], 2), own, number, REQ, E, 2, CAP, 2))(routes_keys, routes_turns).reshape((TOKENS, 2))
    gate_weight = gaussian(keys[10], (E, D, FF), D ** -0.5, 0.078125, ((0, 8), (2, 16)))
    up_weight = gaussian(keys[11], (E, D, FF), D ** -0.5, 0.078125, ((0, 8), (2, 16)))
    down_weight = gaussian(keys[12], (E, FF, D), FF ** -0.5, 0.0625, ((0, 8), (1, 16)))
    return {"queries": queries, "new_kv": new_kv, "kv_cache": kv_cache, "page_table": page_table, "context_lengths": context_lengths, "out_weight": out_weight, "residual_in": residual_in, "norm_gain": norm_gain, "router_weight": router_weight, "routes": routes, "gate_weight": gate_weight, "up_weight": up_weight, "down_weight": down_weight}


EPS = 1e-05

def attend(queries, new_kv, kv_cache, page_table, context_lengths):
    heads_dev = H // N_TP
    group_ids = (jnp.arange(TOKENS, dtype=jnp.int32) // REQ).astype(jnp.int32)
    page_rows = (group_ids[:, None] * POOL + page_table).astype(jnp.int32)
    query_all = queries.astype(jnp.float32).reshape(TOKENS, N_TP, heads_dev, HD)
    live_mask = (jnp.arange(LMAX, dtype=jnp.int32)[None, :] < context_lengths[:, None])[:, None, :]
    score_scale = HD ** (-0.5)

    def one_copy(copy_idx):
        gathered = kv_cache[page_rows, copy_idx].reshape(TOKENS, LMAX, 2 * HD).astype(jnp.float32)
        own_pair = new_kv[:, copy_idx].astype(jnp.float32)
        query_part = query_all[:, copy_idx]
        scores = jnp.einsum('thd,tld->thl', query_part, gathered[:, :, :HD]) * score_scale
        scores = jnp.where(live_mask, scores, -1e+30)
        own_score = jnp.einsum('thd,td->th', query_part, own_pair[:, :HD]) * score_scale
        row_top = jnp.maximum(lax.optimization_barrier(jnp.max(scores, axis=2)), own_score)
        weights = jnp.where(live_mask, jnp.exp(scores - row_top[:, :, None]), 0.0)
        own_weight = jnp.exp(own_score - row_top)
        row_total = lax.optimization_barrier(jnp.sum(weights, axis=2)) + own_weight
        probabilities = lax.optimization_barrier((weights / row_total[:, :, None]).astype(jnp.bfloat16)).astype(jnp.float32)
        own_prob = lax.optimization_barrier((own_weight / row_total).astype(jnp.bfloat16)).astype(jnp.float32)
        mixed_out = jnp.einsum('thl,tld->thd', probabilities, gathered[:, :, HD:])
        mixed_out = mixed_out + own_prob[:, :, None] * own_pair[:, None, HD:]
        return mixed_out.astype(jnp.bfloat16)
    stacked = lax.map(one_copy, jnp.arange(N_TP, dtype=jnp.int32))
    return jnp.transpose(stacked, (1, 0, 2, 3)).reshape(TOKENS, H * HD)

def reference(queries, new_kv, kv_cache, page_table, context_lengths, out_weight, residual_in, norm_gain, router_weight, routes, gate_weight, up_weight, down_weight):
    attn = attend(queries, new_kv, kv_cache, page_table, context_lengths)
    resid = (residual_in.astype(jnp.float32) + jnp.dot(attn, out_weight, preferred_element_type=jnp.float32)).astype(jnp.bfloat16)
    wide_resid = resid.astype(jnp.float32)
    row_scale = lax.rsqrt(lax.optimization_barrier(jnp.mean(wide_resid * wide_resid, axis=1, keepdims=True)) + EPS)
    normed = (wide_resid * row_scale * norm_gain[None, :]).astype(jnp.bfloat16)
    logits = jnp.dot(normed, router_weight, preferred_element_type=jnp.float32)
    first_logit = jnp.take_along_axis(logits, routes[:, 0:1], axis=1)[:, 0]
    second_logit = jnp.take_along_axis(logits, routes[:, 1:2], axis=1)[:, 0]
    weight_first = jax.nn.sigmoid(first_logit - second_logit)
    weight_second = jax.nn.sigmoid(second_logit - first_logit)
    mixture = jnp.zeros((TOKENS, D), jnp.float32)
    picked_count = N_GRP * CAP
    for expert in range(E):
        hit_first = routes[:, 0] == expert
        hit_second = routes[:, 1] == expert
        hit_any = jnp.logical_or(hit_first, hit_second)
        order_ids = jnp.argsort(1 - hit_any.astype(jnp.int32), stable=True)
        picked = order_ids[:picked_count].astype(jnp.int32)
        chosen_rows = normed[picked]
        gate_act = jnp.dot(chosen_rows, gate_weight[expert], preferred_element_type=jnp.float32)
        up_act = jnp.dot(chosen_rows, up_weight[expert], preferred_element_type=jnp.float32)
        hidden = (jax.nn.silu(gate_act) * up_act).astype(jnp.bfloat16)
        result = jnp.dot(hidden, down_weight[expert], preferred_element_type=jnp.float32)
        share = jnp.where(hit_first, weight_first, 0.0) + jnp.where(hit_second, weight_second, 0.0)
        mixture = mixture.at[picked].add(share[picked][:, None] * result)
    return (wide_resid + mixture).astype(jnp.bfloat16)
```

```python
import jax
import jax.numpy as jnp
from jax import lax
from jax.experimental import pallas as pl
from jax.experimental.pallas import tpu as pltpu
from jax.sharding import PartitionSpec as P

F32 = jnp.float32
BF16 = jnp.bfloat16
NEG = -1e30


def attn_kernel(q_ref, own_ref, pt_ref, len_ref, kv_hbm, w_hbm, out_ref, kv, w, cnt, sc, kvsem, wsem):
    pool = kv.shape[0]
    pages = pool // 16
    parts = kvsem.shape[0]
    step = pool // parts
    kv_copies = [
        pltpu.make_async_copy(kv_hbm.at[pl.ds(i * step, step)], kv.at[pl.ds(i * step, step)], kvsem.at[i])
        for i in range(parts)
    ]
    for c in kv_copies:
        c.start()
    wcopy = pltpu.make_async_copy(w_hbm, w, wsem)
    wcopy.start()
    pt = pt_ref[...]
    lens = len_ref[...]
    page_ids = lax.broadcasted_iota(jnp.int32, (pages, 128), 0)
    live = jnp.zeros((pages, 128), jnp.int32)
    for j in range(16):
        here = jnp.clip(lens - 16 * j, 0, 16)
        live = live + jnp.where(page_ids == pt[j : j + 1, :], here, 0)
    cnt[...] = live.astype(F32).astype(BF16)
    q = q_ref[...]
    q2 = jnp.concatenate([q[:, :128], q[:, 128:]], axis=0)
    nt = (((1,), (1,)), ((), ()))
    tn = (((0,), (0,)), ((), ()))
    tok = lax.broadcasted_iota(jnp.int32, (256, 128), 0)
    offs = (tok & 15).astype(F32)
    tok16 = lax.broadcasted_iota(jnp.int32, (256, 16), 0) >> 4
    spread = (tok16 == lax.broadcasted_iota(jnp.int32, (256, 16), 1)).astype(F32).astype(BF16)

    own = own_ref[...]
    s_own = lax.dot_general(own[:, :128], q2, nt, preferred_element_type=F32)
    row = lax.broadcasted_iota(jnp.int32, (128, 128), 0)
    col = lax.broadcasted_iota(jnp.int32, (128, 128), 1)
    eye = row == col
    eye2 = jnp.concatenate([eye.astype(F32), eye.astype(F32)], axis=1) > 0.5
    s_own = jnp.where(eye2, s_own, NEG)
    top = jnp.max(s_own.reshape(16, 8, 256), axis=0)

    per = step // 256

    def pass1(c, top):
        k = kv[pl.ds(pl.multiple_of(c * 256, 256), 256), :128]
        s = lax.dot_general(k, q2, nt, preferred_element_type=F32)
        cn = cnt[pl.ds(pl.multiple_of(c * 16, 16), 16), :]
        m = offs < jnp.dot(spread, cn, preferred_element_type=F32)
        s = jnp.concatenate([jnp.where(m, s[:, :128], NEG), jnp.where(m, s[:, 128:], NEG)], axis=1)
        sc[c] = s
        return jnp.maximum(top, jnp.max(s.reshape(32, 8, 256), axis=0))

    for i in range(parts):
        kv_copies[i].wait()
        top = lax.fori_loop(i * per, (i + 1) * per, pass1, top)
    top = jnp.max(top, axis=0, keepdims=True)
    scale = 128.0 ** -0.5

    p_own = jnp.exp((s_own - top) * scale)
    tot = jnp.sum(p_own.reshape(16, 8, 256), axis=0)
    own_v = jnp.transpose(own_ref[:, 128:].astype(F32))
    acc = jnp.concatenate([own_v, own_v], axis=1) * jnp.sum(p_own, axis=0, keepdims=True)

    def pass2(c, carry):
        tot, acc = carry
        p = jnp.exp((sc[c] - top) * scale)
        tot = tot + jnp.sum(p.reshape(32, 8, 256), axis=0)
        v = kv[pl.ds(pl.multiple_of(c * 256, 256), 256), 128:]
        acc = acc + lax.dot_general(v, p.astype(BF16), tn, preferred_element_type=F32)
        return tot, acc

    tot, acc = lax.fori_loop(0, pool // 256, pass2, (tot, acc))
    tot = jnp.sum(tot, axis=0, keepdims=True)
    att = acc / tot
    attn = jnp.concatenate([jnp.transpose(att[:, :128]), jnp.transpose(att[:, 128:])], axis=1).astype(BF16)
    wcopy.wait()
    cw = out_ref.shape[2]

    def proj(t, _):
        out_ref[t] = jnp.dot(
            attn, w[:, pl.ds(pl.multiple_of(t * cw, 128), cw)], preferred_element_type=F32
        ).astype(BF16)
        return 0

    lax.fori_loop(0, out_ref.shape[0], proj, 0)


def attention_partials(queries, new_kv, kv_cache, page_table, context_lengths, out_weight):
    pool = kv_cache.shape[0] * kv_cache.shape[2]
    vm = pl.BlockSpec(memory_space=pltpu.VMEM)
    hb = pl.BlockSpec(memory_space=pl.ANY)
    return pl.pallas_call(
        attn_kernel,
        out_shape=jax.ShapeDtypeStruct((16, 128, 384), BF16),
        in_specs=[vm, vm, vm, vm, hb, hb],
        out_specs=vm,
        scratch_shapes=[
            pltpu.VMEM((pool, 256), BF16),
            pltpu.VMEM(out_weight.shape, BF16),
            pltpu.VMEM((pool // 16, 128), BF16),
            pltpu.VMEM((pool // 256, 256, 256), F32),
            pltpu.SemaphoreType.DMA((5,)),
            pltpu.SemaphoreType.DMA,
        ],
        compiler_params=pltpu.CompilerParams(vmem_limit_bytes=40 * 1024 * 1024),
        cost_estimate=pl.CostEstimate(flops=1 << 30, bytes_accessed=8 << 20, transcendentals=1 << 21),
        name="attention",
    )(
        queries,
        new_kv.reshape(128, 256),
        page_table.T,
        context_lengths.reshape(1, 128),
        kv_cache.reshape(pool, 256),
        out_weight,
    )


MESH = pl.DeviceIdType.MESH
NT = (((1,), (1,)), ((), ()))
CW = 384
FW = 512
OFFS_OUT = (0, 3, 1, 2)
OFFS_IN = (2, 1, 3, 0)


def route_maps(routes):
    lane = lax.broadcasted_iota(jnp.int32, (128, 128), 1)
    sub = lax.broadcasted_iota(jnp.int32, (128, 128), 0)
    hit0 = (lane == routes[:, 0:1]).astype(F32)
    hit1 = (lane == routes[:, 1:2]).astype(F32)
    hit = hit0 + hit1
    hit_t = jnp.transpose(hit)
    rank = jnp.dot((lane < sub).astype(F32).astype(BF16), hit.astype(BF16), preferred_element_type=F32)
    rank_t = jnp.dot(hit_t.astype(BF16), (sub < lane).astype(F32).astype(BF16), preferred_element_type=F32)
    spot_t = jnp.where(hit_t > 0.5, rank_t, -1.0)
    slot = lax.broadcasted_iota(jnp.int32, (64, 128), 0).astype(F32)
    place = jnp.concatenate([(slot == spot_t[e : e + 1, :]).astype(F32) for e in range(8)], axis=0)
    wide = lax.broadcasted_iota(jnp.int32, (128, 512), 1)

    def back(h, col):
        at = col * 64 + jnp.sum(h * rank, axis=1, keepdims=True).astype(jnp.int32)
        return (wide == at).astype(F32).astype(BF16)

    return place.astype(BF16), back(hit0, routes[:, 0:1]), back(hit1, routes[:, 1:2])


def layer_kernel(
    part_ref, res_ref, gain_ref, router_ref, routes_ref, wg_hbm, wu_hbm, wd_hbm,
    out_ref,
    wg, wu, wd, xg, acc, ssq, hid, p2, rb1, y1, rc1, rb2, y2, rc2,
    rs, xs, ds, fin, ret, stat_out, stat_in, place, back,
    wsem, a1s, a1r, ags, agr, a2s, a2r, ds_s, ds_r, rt_s, rt_r, st_s, st_r,
):
    g = lax.axis_index("grp")
    t = lax.axis_index("tp")
    gy, gc = g // 2, lax.rem(g, 2)
    tz, tx = t // 4, lax.rem(t, 4)
    me = ((tx, tz), (tz, tx))

    def tid(h, c1, c2):
        return c2 * 4 + c1 if h == 0 else c1 * 4 + c2

    def m4(v):
        return lax.rem(v + 4, 4)

    barrier = pltpu.get_barrier_semaphore()

    def greet_t(k, c):
        pl.semaphore_signal(barrier, inc=1, device_id=(g, lax.rem(t + k, 16)), device_id_type=MESH)
        return c

    def greet_g(k, c):
        pl.semaphore_signal(barrier, inc=1, device_id=(lax.rem(g + k, 8), t), device_id_type=MESH)
        return c

    lax.fori_loop(1, 16, greet_t, 0)
    lax.fori_loop(1, 8, greet_g, 0)

    wcopies = [
        pltpu.make_async_copy(src.at[0], dst, wsem.at[i])
        for i, (src, dst) in enumerate(((wg_hbm, wg), (wu_hbm, wu), (wd_hbm, wd)))
    ]
    for c in wcopies:
        c.start()

    pl_m, b0, b1 = route_maps(routes_ref[...])
    place[...] = pl_m
    back[0] = b0
    back[1] = b1

    pl.semaphore_wait(barrier, 22)

    def rcopy(src, dst, ss, rr, dev):
        return pltpu.make_async_remote_copy(
            src_ref=src, dst_ref=dst, send_sem=ss, recv_sem=rr, device_id=dev, device_id_type=MESH
        )

    def reduce_scatter(rows, src, rb, y, rc, ss, rr, produce, finish):
        def q_rows(h, q):
            return pl.ds((2 * h + q) * rows, rows)

        def nbr(h, axis, d):
            c = list(me[h])
            c[axis] = m4(c[axis] + d)
            return (g, tid(h, c[0], c[1]))

        def blk(h, i, d2):
            return tid(h, m4(me[h][0] + OFFS_IN[i]), m4(me[h][1] + d2))

        def msg1(h, i, k, from_buf=None):
            d2, q, d = ((2, 0, 1), (2, 1, -1), (1, 1, 1), (-1, 0, -1), (1, 0, 1), (-1, 1, -1))[k]
            s = src.at[blk(h, i, d2), q_rows(h, q)] if from_buf is None else rb.at[h, i, from_buf]
            n = h * 24 + i * 6 + k
            return rcopy(s, rb.at[h, i, k], ss.at[n], rr.at[n], nbr(h, 1, d))

        def msg2(h, k, i, from_buf=None):
            q, d = ((0, 1), (1, -1), (1, 1), (0, -1), (0, 1), (1, -1))[k]
            s = y.at[h, i, pl.ds(q * rows, rows)] if from_buf is None else rc.at[h, from_buf]
            n = 48 + h * 6 + k
            return rcopy(s, rc.at[h, k], ss.at[n], rr.at[n], nbr(h, 0, d))

        sent = []

        def go(m):
            m.start()
            sent.append(m)

        def stage_g(i):
            produce(i, blk, 0)
            for h in (0, 1):
                go(msg1(h, i, 0))
                go(msg1(h, i, 1))
            produce(i, blk, 1)
            for h in (0, 1):
                go(msg1(h, i, 2))
                go(msg1(h, i, 3))

        def stage_h(i):
            for h in (0, 1):
                msg1(h, i, 0).wait_recv()
                rb[h, i, 0] = (
                    rb[h, i, 0].astype(F32) + src[blk(h, i, 1), q_rows(h, 0)].astype(F32)
                ).astype(BF16)
                go(msg1(h, i, 4, 0))
                msg1(h, i, 1).wait_recv()
                rb[h, i, 1] = (
                    rb[h, i, 1].astype(F32) + src[blk(h, i, -1), q_rows(h, 1)].astype(F32)
                ).astype(BF16)
                go(msg1(h, i, 5, 1))

        def stage_j(i):
            produce(i, blk, 2)
            for h in (0, 1):
                for q, (k1, k2) in ((0, (3, 4)), (1, (2, 5))):
                    msg1(h, i, k1).wait_recv()
                    msg1(h, i, k2).wait_recv()
                    y[h, i, pl.ds(q * rows, rows)] = (
                        src[blk(h, i, 0), q_rows(h, q)].astype(F32)
                        + rb[h, i, k1].astype(F32)
                        + rb[h, i, k2].astype(F32)
                    ).astype(BF16)
                    if i == 0:
                        go(msg2(h, q, 0))
                if i == 1:
                    go(msg2(h, 2, 1))
                    msg2(h, 0, 1).wait_recv()
                    rc[h, 0] = (rc[h, 0].astype(F32) + y[h, 1, pl.ds(0, rows)].astype(F32)).astype(BF16)
                    go(msg2(h, 4, 1, 0))
                if i == 2:
                    go(msg2(h, 3, 2))
                    msg2(h, 1, 2).wait_recv()
                    rc[h, 1] = (rc[h, 1].astype(F32) + y[h, 2, pl.ds(rows, rows)].astype(F32)).astype(BF16)
                    go(msg2(h, 5, 2, 1))

        stage_g(0)
        stage_g(1)
        stage_h(0)
        stage_j(0)
        stage_g(2)
        stage_h(1)
        stage_j(1)
        stage_g(3)
        stage_h(2)
        stage_j(2)
        stage_h(3)
        stage_j(3)
        for h in (0, 1):
            for q, (k1, k2) in ((0, (3, 4)), (1, (2, 5))):
                msg2(h, k1, 3).wait_recv()
                msg2(h, k2, 3).wait_recv()
                finish(
                    h,
                    q,
                    y[h, 3, pl.ds(q * rows, rows)].astype(F32)
                    + rc[h, k1].astype(F32)
                    + rc[h, k2].astype(F32),
                )
        return sent

    gain_row = gain_ref[pl.ds(t, 1), :]

    def finish1(h, q, v):
        at = pl.ds((2 * h + q) * 32, 32)
        r = (res_ref[at, :].astype(F32) + v).astype(BF16)
        rs[at, :] = r
        xs[at, :] = (r.astype(F32) * gain_row).astype(BF16)

    sent1 = reduce_scatter(32, part_ref, rb1, y1, rc1, a1s, a1r, lambda i, blk, s: None, finish1)

    x = xs[...]
    ds[...] = jnp.dot(place[...], x, preferred_element_type=F32).astype(BF16).reshape(8, 64, CW)

    def seat(src_y, src_c, dst_y):
        r = m4(src_y - dst_y)
        p = lax.rem(r, 2) * 2 + r // 2
        return pl.multiple_of(p * 128 + src_c * 64, 64), p * 2 + src_c

    own_row, own_slot = seat(gy, gc, gy)
    xg[t, pl.ds(own_row, 64), :] = ds[g]

    def deal(k):
        e = lax.rem(g + k, 8)
        row, slot = seat(gy, gc, e // 2)
        return rcopy(ds.at[e], xg.at[t, pl.ds(row, 64)], ds_s.at[k], ds_r.at[slot], (e, t))

    def deal_start(k, c):
        deal(k).start()
        return c

    lax.fori_loop(1, 8, deal_start, 0)

    def dealt(slot):
        at = xg.at[t, pl.ds(pl.multiple_of(slot * 64, 64), 64)]
        return rcopy(at, at, ds_s.at[0], ds_r.at[slot], (g, t))

    lane8 = lax.broadcasted_iota(jnp.int32, (128, 8), 1)
    sign = (lane8 == routes_ref[:, 0:1]).astype(F32) - (lane8 == routes_ref[:, 1:2]).astype(F32)
    logit = jnp.dot(x, router_ref[t], preferred_element_type=F32)
    diff = jnp.sum(logit * sign, axis=1, keepdims=True)
    r32 = rs[...].astype(F32)
    sq = jnp.sum(r32 * r32, axis=1, keepdims=True)
    lane = lax.broadcasted_iota(jnp.int32, (128, 128), 1)
    tile = jnp.where(lane == 0, diff, jnp.where(lane == 1, sq, 0.0))
    tile = jnp.transpose(tile)[:8, :]
    stat_out[...] = tile
    stat_in[0] = tile

    def stat(k):
        return rcopy(stat_out, stat_in.at[k], st_s.at[k], st_r.at[k], (g, lax.rem(t + k, 16)))

    def stat_start(k, c):
        stat(k).start()
        return c

    lax.fori_loop(1, 16, stat_start, 0)

    ag_sent = []

    def ag(h, phase, i, k, b):
        q, d = ((0, 1), (1, 1), (0, -1), (1, -1), (0, 1), (1, -1))[k]
        c = list(me[h])
        c[phase] = m4(c[phase] + d)
        ref = xg.at[b, pl.ds((2 * h + q) * 128, 128)]
        n = h * 30 + phase * 6 + i * 6 + k
        return rcopy(ref, ref, ags.at[n], agr.at[n], (g, tid(h, c[0], c[1])))

    def send(*a):
        m = ag(*a)
        m.start()
        ag_sent.append(m)

    def ab(h, o1, o2):
        return tid(h, m4(me[h][0] + o1), m4(me[h][1] + o2))

    def wait(h, phase, i, k, b):
        ag(h, phase, i, k, b).wait_recv()

    def spread(h, i, q):
        b = ab(h, OFFS_OUT[i], 0)
        send(h, 1, i, q, b)
        send(h, 1, i, 2 + q, b)

    def own_quarter(h, q):
        p = 2 * h + q
        for c in (0, 1):
            slot = p * 2 + c
            if p == 0:

                @pl.when(gc != c)
                def _():
                    dealt(slot).wait_recv()

            else:
                dealt(slot).wait_recv()
        send(h, 0, 0, q, t)
        send(h, 0, 0, 2 + q, t)
        spread(h, 0, q)

    def stage_p(i, h):
        if i == 1:
            b = ab(h, -1, 0)
            wait(h, 0, 0, 0, b)
            send(h, 0, 0, 4, b)
            spread(h, i, 0)
            wait(h, 0, 0, 1, b)
            spread(h, i, 1)
        elif i == 2:
            b = ab(h, 1, 0)
            wait(h, 0, 0, 3, b)
            send(h, 0, 0, 5, b)
            spread(h, i, 1)
            wait(h, 0, 0, 2, b)
            spread(h, i, 0)
        elif i == 3:
            b = ab(h, 2, 0)
            wait(h, 0, 0, 4, b)
            spread(h, i, 0)
            wait(h, 0, 0, 5, b)
            spread(h, i, 1)

    def stage_f(i, h):
        b = ab(h, OFFS_OUT[i], -1)
        wait(h, 1, i, 0, b)
        send(h, 1, i, 4, b)
        b = ab(h, OFFS_OUT[i], 1)
        wait(h, 1, i, 3, b)
        send(h, 1, i, 5, b)

    def stage_w1(i, h):
        wait(h, 1, i, 1, ab(h, OFFS_OUT[i], -1))
        wait(h, 1, i, 2, ab(h, OFFS_OUT[i], 1))

    def stage_w2(i, h):
        b = ab(h, OFFS_OUT[i], 2)
        wait(h, 1, i, 4, b)
        wait(h, 1, i, 5, b)

    def eat(o1, lo, hi):
        def body(n, c):
            h = lax.rem(n, 2)
            j = n // 2
            o2 = jnp.where(j == 0, 0, jnp.where(j == 1, 3, j - 1))
            c1 = m4(jnp.where(h == 0, tx, tz) + o1)
            c2 = m4(jnp.where(h == 0, tz, tx) + o2)
            b = jnp.where(h == 0, c2 * 4 + c1, c1 * 4 + c2)
            xb = xg[b, pl.ds(pl.multiple_of(h * 256, 256), 256), :]
            wat = pl.ds(pl.multiple_of(b * CW, CW), CW)
            acc[h, 0] += jnp.dot(xb, wg[wat, :], preferred_element_type=F32)
            acc[h, 1] += jnp.dot(xb, wu[wat, :], preferred_element_type=F32)
            v = xb.astype(F32) / gain_ref[pl.ds(b, 1), :]
            v = v * v
            ssq[h] += v[:, :128] + v[:, 128:256] + v[:, 256:]
            return c

        lax.fori_loop(lo * 2, hi * 2, body, 0)

    own_quarter(0, 0)
    acc[...] = jnp.zeros_like(acc)
    ssq[...] = jnp.zeros_like(ssq)
    own_quarter(1, 0)
    own_quarter(1, 1)
    own_quarter(0, 1)
    for h in (0, 1):
        stage_p(1, h)
    for h in (0, 1):
        stage_p(2, h)
    for h in (0, 1):
        stage_f(0, h)
    for h in (0, 1):
        stage_p(3, h)
    for h in (0, 1):
        stage_f(1, h)
    wcopies[0].wait()
    wcopies[1].wait()
    for i in (0, 1, 2, 3):
        for h in (0, 1):
            stage_w1(i, h)
        if i == 3:
            eat(OFFS_OUT[i], 0, 3)
        for h in (0, 1):
            stage_w2(i, h)
        if i < 2:
            for h in (0, 1):
                stage_f(i + 2, h)
        if i == 3:
            eat(OFFS_OUT[i], 3, 4)
        else:
            eat(OFFS_OUT[i], 0, 4)

    for h in (0, 1):
        total = jnp.sum(ssq[h], axis=1, keepdims=True)
        sc = lax.rsqrt(total / (16.0 * CW) + 1e-5)
        gate = acc[h, 0] * sc
        up = acc[h, 1] * sc
        hid[h] = (gate / (1.0 + jnp.exp(-gate)) * up).astype(BF16)
    wcopies[2].wait()

    def produce(i, blk, stage):
        todo = ((2,), (1, -1), (0,))[stage]
        for h in (0, 1):
            hv = hid[h]
            for d2 in todo:
                b = blk(h, i, d2)
                p2[b, h * 256 : (h + 1) * 256, :] = jnp.dot(
                    hv, wd[:, pl.ds(pl.multiple_of(b * CW, 128), CW)], preferred_element_type=F32
                ).astype(BF16)

    def back_copy(slot):
        p = slot // 2
        r = lax.rem(p, 2) * 2 + p // 2
        dst = lax.rem(gy + r, 4) * 2 + lax.rem(slot, 2)
        return rcopy(
            fin.at[pl.ds(pl.multiple_of(slot * 64, 64), 64)],
            ret.at[pl.ds(pl.multiple_of(g * 64, 64), 64)],
            rt_s.at[slot],
            rt_r.at[g],
            (dst, t),
        )

    def finish2(h, q, v):
        p = 2 * h + q
        fin[p * 128 : (p + 1) * 128, :] = v.astype(BF16)
        for c in (0, 1):
            slot = p * 2 + c
            if p == 0:

                @pl.when(gc != c)
                def _():
                    back_copy(slot).start()

                @pl.when(gc == c)
                def _():
                    ret[pl.ds(pl.multiple_of(g * 64, 64), 64), :] = fin[slot * 64 : slot * 64 + 64, :]

            else:
                back_copy(slot).start()

    sent2 = reduce_scatter(128, p2, rb2, y2, rc2, a2s, a2r, produce, finish2)

    def stat_wait(k, c):
        stat(k).wait_recv()
        return c

    lax.fori_loop(1, 16, stat_wait, 0)
    sums = jnp.sum(stat_in[...], axis=0)
    diff_all = sums[0:1, :] * lax.rsqrt(sums[1:2, :] / (16.0 * CW) + 1e-5)
    tile = jnp.transpose(jnp.broadcast_to(diff_all, (128, 128)))
    dcol = tile[:, 0:1]
    wa = 1.0 / (1.0 + jnp.exp(-dcol))
    wb = 1.0 / (1.0 + jnp.exp(dcol))

    def ret_wait(k, c):
        e = lax.rem(g + k, 8)
        at = ret.at[pl.ds(pl.multiple_of(e * 64, 64), 64)]
        rcopy(at, at, rt_s.at[0], rt_r.at[e], (g, t)).wait_recv()
        return c

    lax.fori_loop(1, 8, ret_wait, 0)
    rv = ret[...]
    out_ref[...] = (
        rs[...].astype(F32)
        + wa * jnp.dot(back[0], rv, preferred_element_type=F32)
        + wb * jnp.dot(back[1], rv, preferred_element_type=F32)
    ).astype(BF16)

    for m in sent1 + ag_sent + sent2:
        m.wait_send()

    def stat_sent(k, c):
        stat(k).wait_send()
        return c

    def deal_sent(k, c):
        deal(k).wait_send()
        return c

    lax.fori_loop(1, 16, stat_sent, 0)
    lax.fori_loop(1, 8, deal_sent, 0)
    for slot in range(8):
        if slot < 2:

            @pl.when(gc != slot)
            def _():
                back_copy(slot).wait_send()

        else:
            back_copy(slot).wait_send()


def layer(part, residual_in, norm_gain, router_weight, routes, gate_weight, up_weight, down_weight):
    vm = pl.BlockSpec(memory_space=pltpu.VMEM)
    hb = pl.BlockSpec(memory_space=pl.ANY)
    dma = pltpu.SemaphoreType.DMA
    return pl.pallas_call(
        layer_kernel,
        out_shape=jax.ShapeDtypeStruct((128, CW), BF16),
        in_specs=[vm, vm, vm, vm, vm, hb, hb, hb],
        out_specs=vm,
        scratch_shapes=[
            pltpu.VMEM((16 * CW, FW), BF16),
            pltpu.VMEM((16 * CW, FW), BF16),
            pltpu.VMEM((FW, 16 * CW), BF16),
            pltpu.VMEM((16, 512, CW), BF16),
            pltpu.VMEM((2, 2, 256, FW), F32),
            pltpu.VMEM((2, 256, 128), F32),
            pltpu.VMEM((2, 256, FW), BF16),
            pltpu.VMEM((16, 512, CW), BF16),
            pltpu.VMEM((2, 4, 6, 32, CW), BF16),
            pltpu.VMEM((2, 4, 64, CW), BF16),
            pltpu.VMEM((2, 6, 32, CW), BF16),
            pltpu.VMEM((2, 4, 6, 128, CW), BF16),
            pltpu.VMEM((2, 4, 256, CW), BF16),
            pltpu.VMEM((2, 6, 128, CW), BF16),
            pltpu.VMEM((128, CW), BF16),
            pltpu.VMEM((128, CW), BF16),
            pltpu.VMEM((8, 64, CW), BF16),
            pltpu.VMEM((512, CW), BF16),
            pltpu.VMEM((512, CW), BF16),
            pltpu.VMEM((8, 128), F32),
            pltpu.VMEM((16, 8, 128), F32),
            pltpu.VMEM((512, 128), BF16),
            pltpu.VMEM((2, 128, 512), BF16),
            dma((3,)),
            dma((60,)),
            dma((60,)),
            dma((60,)),
            dma((60,)),
            dma((60,)),
            dma((60,)),
            dma((8,)),
            dma((8,)),
            dma((8,)),
            dma((8,)),
            dma((16,)),
            dma((16,)),
        ],
        compiler_params=pltpu.CompilerParams(
            collective_id=0, has_side_effects=True, vmem_limit_bytes=60 * 1024 * 1024
        ),
        cost_estimate=pl.CostEstimate(flops=10 << 30, bytes_accessed=24 << 20, transcendentals=1 << 18),
        name="layer",
    )(
        part,
        residual_in,
        norm_gain.reshape(16, CW),
        router_weight.reshape(16, CW, 8),
        routes,
        gate_weight,
        up_weight,
        down_weight,
    )


def local(
    queries, new_kv, kv_cache, page_table, context_lengths, out_weight, residual_in,
    norm_gain, router_weight, routes, gate_weight, up_weight, down_weight,
):
    part = attention_partials(queries, new_kv, kv_cache, page_table, context_lengths, out_weight)
    return layer(part, residual_in, norm_gain, router_weight, routes, gate_weight, up_weight, down_weight)


def solution(mesh):
    return jax.shard_map(
        local,
        mesh=mesh,
        in_specs=(
            P("grp", "tp"),
            P("grp", "tp", None),
            P("grp", "tp", None, None),
            P("grp", None),
            P("grp"),
            P("tp", None),
            P("grp", "tp"),
            P(),
            P(),
            P("grp", None),
            P("grp", None, "tp"),
            P("grp", None, "tp"),
            P("grp", "tp", None),
        ),
        out_specs=P("grp", "tp"),
        check_vma=False,
    )
```

```python
import jax
import jax.numpy as jnp
from jax import lax
from jax.experimental import pallas as pl
from jax.experimental.pallas import tpu as pltpu
from jax.sharding import PartitionSpec as P

F32 = jnp.float32
BF16 = jnp.bfloat16
MESH = pl.DeviceIdType.MESH
NT = (((1,), (1,)), ((), ()))
TN = (((0,), (0,)), ((), ()))
PARTS = 5
NEG = -1e30
CW = 384
FW = 512
OFFS_OUT = (0, 3, 1, 2)
OFFS_IN = (2, 1, 3, 0)


def attend(q, own, live_ref, kv, kv_copies, part_rows):
    q2 = jnp.concatenate([q[:, :128], q[:, 128:]], axis=0)
    pages = part_rows // 16
    tok = lax.broadcasted_iota(jnp.int32, (256, 128), 0)
    offs = (tok & 15).astype(F32)
    tok16 = lax.broadcasted_iota(jnp.int32, (256, 16), 0) >> 4
    spread = (tok16 == lax.broadcasted_iota(jnp.int32, (256, 16), 1)).astype(F32).astype(BF16)
    s_own = lax.dot_general(own[:, :128], q2, NT, preferred_element_type=F32)
    row = lax.broadcasted_iota(jnp.int32, (128, 128), 0)
    col = lax.broadcasted_iota(jnp.int32, (128, 128), 1)
    eye = (row == col).astype(F32)
    eye = jnp.concatenate([eye, eye], axis=1)
    top = jnp.sum(s_own * eye, axis=0, keepdims=True)
    tot = jnp.ones((8, 256), F32) * 0.125
    own_v = jnp.transpose(own[:, 128:].astype(F32))
    acc = jnp.concatenate([own_v, own_v], axis=1)
    scale = 128.0 ** -0.5
    for i, copy in enumerate(kv_copies):
        copy.wait()
        tiles = []
        peak = top
        for c in range(part_rows // 256):
            at = i * part_rows + c * 256
            s = lax.dot_general(kv[at : at + 256, :128], q2, NT, preferred_element_type=F32)
            cn = live_ref[i * pages + c * 16 : i * pages + c * 16 + 16, :]
            m = offs < jnp.dot(spread, cn, preferred_element_type=F32)
            s = jnp.concatenate([jnp.where(m, s[:, :128], NEG), jnp.where(m, s[:, 128:], NEG)], axis=1)
            tiles.append(s)
            peak = jnp.maximum(peak, jnp.max(jnp.max(s.reshape(32, 8, 256), axis=0), axis=0, keepdims=True))
        fade = jnp.exp((top - peak) * scale)
        top = peak
        tot = tot * fade
        ps = []
        for s in tiles:
            p = jnp.exp((s - top) * scale)
            tot = tot + jnp.sum(p.reshape(32, 8, 256), axis=0)
            ps.append(p.astype(BF16))
        p = jnp.concatenate(ps, axis=0)
        acc = acc * fade + lax.dot_general(
            kv[i * part_rows : (i + 1) * part_rows, 128:], p, TN, preferred_element_type=F32
        )
    att = acc / jnp.sum(tot, axis=0, keepdims=True)
    return jnp.concatenate([jnp.transpose(att[:, :128]), jnp.transpose(att[:, 128:])], axis=1).astype(BF16)


def as_column(row):
    return jnp.transpose(jnp.broadcast_to(row, (128, 128)))[:, 0:1]


def route_maps(routes):
    lane = lax.broadcasted_iota(jnp.int32, (128, 128), 1)
    sub = lax.broadcasted_iota(jnp.int32, (128, 128), 0)
    hit0 = (sub == routes[0:1, :]).astype(F32)
    hit1 = (sub == routes[1:2, :]).astype(F32)
    hit = hit0 + hit1
    rank = jnp.dot(hit.astype(BF16), (sub < lane).astype(F32).astype(BF16), preferred_element_type=F32)
    spot = jnp.where(hit > 0.5, rank, -1.0)
    slot = lax.broadcasted_iota(jnp.int32, (64, 128), 0).astype(F32)
    place = jnp.concatenate([(slot == spot[e : e + 1, :]).astype(F32) for e in range(8)], axis=0)
    wide = lax.broadcasted_iota(jnp.int32, (128, 512), 1).astype(F32)

    def back(h, r):
        at = r.astype(F32) * 64.0 + jnp.sum(h * rank, axis=0, keepdims=True)
        return (wide == as_column(at)).astype(F32).astype(BF16)

    sign = hit0[:8, :] - hit1[:8, :]
    return place.astype(BF16), back(hit0, routes[0:1, :]), back(hit1, routes[1:2, :]), sign


def layer_kernel(
    q_hbm, own_hbm, pt_hbm, len_hbm, kv_hbm, w_hbm, res_hbm, gain_hbm, router_hbm, routes_hbm, wg_hbm, wu_hbm, wd_hbm,
    out_ref,
    q_ref, own_ref, pt_ref, len_ref, kv, w, res_ref, gain_ref, router_ref, routes_ref, live, part, ginv,
    wg, wu, wd, xg, acc, ssq, hid, p2, rb1, y1, rc1, rb2, y2, rc2,
    rs, xs, ds, fin, ret, stat_out, stat_in, place, back,
    ksem, msem, wsem, a1s, a1r, ags, agr, a2s, a2r, ds_s, ds_r, rt_s, rt_r, st_s, st_r,
):
    g = lax.axis_index("grp")
    t = lax.axis_index("tp")
    gy, gc = g // 2, lax.rem(g, 2)
    tz, tx = t // 4, lax.rem(t, 4)
    me = ((tx, tz), (tz, tx))

    def tid(h, c1, c2):
        return c2 * 4 + c1 if h == 0 else c1 * 4 + c2

    def m4(v):
        return lax.rem(v + 4, 4)

    barrier = pltpu.get_barrier_semaphore()

    def greet_t(k, c):
        pl.semaphore_signal(barrier, inc=1, device_id=(g, lax.rem(t + k, 16)), device_id_type=MESH)
        return c

    def greet_g(k, c):
        pl.semaphore_signal(barrier, inc=1, device_id=(lax.rem(g + k, 8), t), device_id_type=MESH)
        return c

    lax.fori_loop(1, 16, greet_t, 0)
    lax.fori_loop(1, 8, greet_g, 0)

    step = kv.shape[0] // PARTS
    small = [
        pltpu.make_async_copy(src, dst, msem.at[i])
        for i, (src, dst) in enumerate(
            (
                (pt_hbm, pt_ref), (len_hbm, len_ref), (q_hbm, q_ref), (own_hbm, own_ref), (routes_hbm, routes_ref),
                (res_hbm, res_ref), (gain_hbm, gain_ref), (router_hbm, router_ref), (w_hbm, w),
            )
        )
    ]
    kv_copies = [
        pltpu.make_async_copy(kv_hbm.at[pl.ds(i * step, step)], kv.at[pl.ds(i * step, step)], ksem.at[i])
        for i in range(PARTS)
    ]
    wcopies = [
        pltpu.make_async_copy(src.at[0], dst, wsem.at[i])
        for i, (src, dst) in enumerate(((wg_hbm, wg), (wu_hbm, wu), (wd_hbm, wd)))
    ]
    for c in small[:5] + kv_copies + small[5:] + wcopies:
        c.start()

    small[0].wait()
    small[1].wait()
    pages = live.shape[0]
    page_ids = lax.broadcasted_iota(jnp.int32, (pages, 128), 0)
    lens = len_ref[...]
    count = jnp.zeros((pages, 128), jnp.int32)
    for j in range(16):
        here = jnp.clip(lens - 16 * j, 0, 16)
        count = count + jnp.where(page_ids == pt_ref[j : j + 1, :], here, 0)
    live[...] = count.astype(F32).astype(BF16)
    small[4].wait()
    pl_m, b0, b1, sign = route_maps(routes_ref[...])
    place[...] = pl_m
    back[0] = b0
    back[1] = b1
    small[2].wait()
    small[3].wait()
    attn = attend(q_ref[...], own_ref[...], live, kv, kv_copies, step)
    for c in small[5:]:
        c.wait()
    ginv[...] = 1.0 / gain_ref[...]

    pl.semaphore_wait(barrier, 22)

    def rcopy(src, dst, ss, rr, dev):
        return pltpu.make_async_remote_copy(
            src_ref=src, dst_ref=dst, send_sem=ss, recv_sem=rr, device_id=dev, device_id_type=MESH
        )

    def reduce_scatter(rows, src, rb, y, rc, ss, rr, produce, finish):
        def q_rows(h, q):
            return pl.ds((2 * h + q) * rows, rows)

        def nbr(h, axis, d):
            c = list(me[h])
            c[axis] = m4(c[axis] + d)
            return (g, tid(h, c[0], c[1]))

        def blk(h, i, d2):
            return tid(h, m4(me[h][0] + OFFS_IN[i]), m4(me[h][1] + d2))

        def msg1(h, i, k, from_buf=None):
            d2, q, d = ((2, 0, 1), (2, 1, -1), (1, 1, 1), (-1, 0, -1), (1, 0, 1), (-1, 1, -1))[k]
            s = src.at[blk(h, i, d2), q_rows(h, q)] if from_buf is None else rb.at[h, i, from_buf]
            n = h * 24 + i * 6 + k
            return rcopy(s, rb.at[h, i, k], ss.at[n], rr.at[n], nbr(h, 1, d))

        def msg2(h, k, i, from_buf=None):
            q, d = ((0, 1), (1, -1), (1, 1), (0, -1), (0, 1), (1, -1))[k]
            s = y.at[h, i, pl.ds(q * rows, rows)] if from_buf is None else rc.at[h, from_buf]
            n = 48 + h * 6 + k
            return rcopy(s, rc.at[h, k], ss.at[n], rr.at[n], nbr(h, 0, d))

        sent = []

        def go(m):
            m.start()
            sent.append(m)

        def stage_g(i):
            produce(i, blk, 0)
            for h in (0, 1):
                go(msg1(h, i, 0))
                go(msg1(h, i, 1))
            produce(i, blk, 1)
            for h in (0, 1):
                go(msg1(h, i, 2))
                go(msg1(h, i, 3))

        def stage_h(i):
            for h in (0, 1):
                msg1(h, i, 0).wait_recv()
                rb[h, i, 0] = (
                    rb[h, i, 0].astype(F32) + src[blk(h, i, 1), q_rows(h, 0)].astype(F32)
                ).astype(BF16)
                go(msg1(h, i, 4, 0))
                msg1(h, i, 1).wait_recv()
                rb[h, i, 1] = (
                    rb[h, i, 1].astype(F32) + src[blk(h, i, -1), q_rows(h, 1)].astype(F32)
                ).astype(BF16)
                go(msg1(h, i, 5, 1))

        def stage_j(i):
            produce(i, blk, 2)
            for h in (0, 1):
                for q, (k1, k2) in ((0, (3, 4)), (1, (2, 5))):
                    msg1(h, i, k1).wait_recv()
                    msg1(h, i, k2).wait_recv()
                    y[h, i, pl.ds(q * rows, rows)] = (
                        src[blk(h, i, 0), q_rows(h, q)].astype(F32)
                        + rb[h, i, k1].astype(F32)
                        + rb[h, i, k2].astype(F32)
                    ).astype(BF16)
                    if i == 0:
                        go(msg2(h, q, 0))
                if i == 1:
                    go(msg2(h, 2, 1))
                    msg2(h, 0, 1).wait_recv()
                    rc[h, 0] = (rc[h, 0].astype(F32) + y[h, 1, pl.ds(0, rows)].astype(F32)).astype(BF16)
                    go(msg2(h, 4, 1, 0))
                if i == 2:
                    go(msg2(h, 3, 2))
                    msg2(h, 1, 2).wait_recv()
                    rc[h, 1] = (rc[h, 1].astype(F32) + y[h, 2, pl.ds(rows, rows)].astype(F32)).astype(BF16)
                    go(msg2(h, 5, 2, 1))

        stage_g(0)
        stage_g(1)
        stage_h(0)
        stage_g(2)
        stage_h(1)
        stage_j(0)
        stage_g(3)
        stage_h(2)
        stage_j(1)
        stage_h(3)
        stage_j(2)
        stage_j(3)
        for h in (0, 1):
            for q, (k1, k2) in ((0, (3, 4)), (1, (2, 5))):
                msg2(h, k1, 3).wait_recv()
                msg2(h, k2, 3).wait_recv()
                finish(
                    h,
                    q,
                    y[h, 3, pl.ds(q * rows, rows)].astype(F32)
                    + rc[h, k1].astype(F32)
                    + rc[h, k2].astype(F32),
                )
        return sent

    sent1 = []

    def project(n, c):
        def third(v):
            return v + (v == 2).astype(jnp.int32)

        m = n - 7
        ox = jnp.where(n < 4, 2, jnp.where(n < 7, third(n - 4), third(m // 3)))
        oz = jnp.where(n < 4, n, jnp.where(n < 7, 2, third(lax.rem(m, 3))))
        b = m4(tz + oz) * 4 + m4(tx + ox)
        part[b] = jnp.dot(
            attn, w[:, pl.ds(pl.multiple_of(b * CW, 128), CW)], preferred_element_type=F32
        ).astype(BF16)
        return c

    def far(h, axis, o):
        c = list(me[h])
        c[axis] = m4(c[axis] + o)
        return (g, tid(h, c[0], c[1]))

    def out1(h, i, k):
        o1, o2 = OFFS_IN[i], (2, 1, -1)[k]
        n = h * 12 + i * 3 + k
        return rcopy(
            part.at[tid(h, m4(me[h][0] + o1), m4(me[h][1] + o2)), pl.ds(h * 64, 64)],
            rb1.at[h, i, k], a1s.at[n], a1r.at[n], far(h, 1, o2),
        )

    def out2(h, i):
        n = 24 + h * 3 + i
        return rcopy(y1.at[h, i], rc1.at[h, i], a1s.at[n], a1r.at[n], far(h, 0, OFFS_IN[i]))

    def go1(m):
        m.start()
        sent1.append(m)

    lax.fori_loop(0, 7, project, 0)
    for k in range(3):
        for h in (0, 1):
            go1(out1(h, 0, k))
    lax.fori_loop(7, 16, project, 0)
    for i in (1, 2, 3):
        for k in range(3):
            for h in (0, 1):
                go1(out1(h, i, k))
    gain_row = gain_ref[:, pl.ds(pl.multiple_of(t * CW, 128), CW)]
    for i in range(4):
        for h in (0, 1):
            for k in range(3):
                out1(h, i, k).wait_recv()
            v = part[tid(h, m4(me[h][0] + OFFS_IN[i]), me[h][1]), h * 64 : h * 64 + 64, :].astype(F32)
            for k in range(3):
                v = v + rb1[h, i, k].astype(F32)
            if i < 3:
                y1[h, i] = v.astype(BF16)
                go1(out2(h, i))
            else:
                for k in range(3):
                    out2(h, k).wait_recv()
                    v = v + rc1[h, k].astype(F32)
                at = pl.ds(h * 64, 64)
                r = (res_ref[at, :].astype(F32) + v).astype(BF16)
                rs[at, :] = r
                xs[at, :] = (r.astype(F32) * gain_row).astype(BF16)

    x = xs[...]
    ds[...] = jnp.dot(place[...], x, preferred_element_type=F32).astype(BF16).reshape(8, 64, CW)

    def seat(src_y, src_c, dst_y):
        r = m4(src_y - dst_y)
        p = lax.rem(r, 2) * 2 + r // 2
        return pl.multiple_of(p * 128 + src_c * 64, 64), p * 2 + src_c

    own_row, own_slot = seat(gy, gc, gy)
    xg[t, pl.ds(own_row, 64), :] = ds[g]

    def deal(k):
        e = lax.rem(g + k, 8)
        row, slot = seat(gy, gc, e // 2)
        return rcopy(ds.at[e], xg.at[t, pl.ds(row, 64)], ds_s.at[k], ds_r.at[slot], (e, t))

    def deal_start(k, c):
        deal(k).start()
        return c

    lax.fori_loop(1, 8, deal_start, 0)

    def dealt(slot):
        at = xg.at[t, pl.ds(pl.multiple_of(slot * 64, 64), 64)]
        return rcopy(at, at, ds_s.at[0], ds_r.at[slot], (g, t))

    logit = lax.dot_general(
        router_ref[:, pl.ds(pl.multiple_of(t * CW, 128), CW)], x, NT, preferred_element_type=F32
    )
    diff = jnp.sum(logit * sign, axis=0, keepdims=True)
    r32 = rs[...].astype(F32)
    sq = jnp.sum(r32 * r32, axis=1, keepdims=True)
    sq = jnp.transpose(jnp.broadcast_to(sq, (128, 128)))[:8, :]
    sub8 = lax.broadcasted_iota(jnp.int32, (8, 128), 0)
    tile = jnp.where(sub8 == 0, diff, jnp.where(sub8 == 1, sq, 0.0))
    stat_out[...] = tile
    stat_in[0] = tile

    def stat(k):
        return rcopy(stat_out, stat_in.at[k], st_s.at[k], st_r.at[k], (g, lax.rem(t + k, 16)))

    def stat_start(k, c):
        stat(k).start()
        return c

    lax.fori_loop(1, 16, stat_start, 0)

    ag_sent = []

    def ag(h, phase, i, k, b):
        q, d = ((0, 1), (1, 1), (0, -1), (1, -1), (0, 1), (1, -1))[k]
        c = list(me[h])
        c[phase] = m4(c[phase] + d)
        ref = xg.at[b, pl.ds((2 * h + q) * 128, 128)]
        n = h * 30 + phase * 6 + i * 6 + k
        return rcopy(ref, ref, ags.at[n], agr.at[n], (g, tid(h, c[0], c[1])))

    def send(*a):
        m = ag(*a)
        m.start()
        ag_sent.append(m)

    def ab(h, o1, o2):
        return tid(h, m4(me[h][0] + o1), m4(me[h][1] + o2))

    def wait(h, phase, i, k, b):
        ag(h, phase, i, k, b).wait_recv()

    def spread(h, i, q):
        b = ab(h, OFFS_OUT[i], 0)
        send(h, 1, i, q, b)
        send(h, 1, i, 2 + q, b)

    def own_quarter(h, q):
        p = 2 * h + q
        for c in (0, 1):
            slot = p * 2 + c
            if p == 0:

                @pl.when(gc != c)
                def _():
                    dealt(slot).wait_recv()

            else:
                dealt(slot).wait_recv()
        send(h, 0, 0, q, t)
        send(h, 0, 0, 2 + q, t)

    def stage_f(i):
        for h in (0, 1):
            b = ab(h, OFFS_OUT[i], -1)
            wait(h, 1, i, 0, b)
            send(h, 1, i, 4, b)
            b = ab(h, OFFS_OUT[i], 1)
            wait(h, 1, i, 3, b)
            send(h, 1, i, 5, b)

    def stage_w1(i):
        for h in (0, 1):
            wait(h, 1, i, 1, ab(h, OFFS_OUT[i], -1))
            wait(h, 1, i, 2, ab(h, OFFS_OUT[i], 1))

    def stage_w2(i):
        for h in (0, 1):
            b = ab(h, OFFS_OUT[i], 2)
            wait(h, 1, i, 4, b)
            wait(h, 1, i, 5, b)

    def eat(*offsets):
        def body(n, c):
            h = lax.rem(n, 2)
            j = n // 2
            o1, o2 = offsets[0]
            for m, (u1, u2) in enumerate(offsets):
                o1 = jnp.where(j == m, u1, o1)
                o2 = jnp.where(j == m, u2, o2)
            c1 = m4(jnp.where(h == 0, tx, tz) + o1)
            c2 = m4(jnp.where(h == 0, tz, tx) + o2)
            b = jnp.where(h == 0, c2 * 4 + c1, c1 * 4 + c2)
            xb = xg[b, pl.ds(pl.multiple_of(h * 256, 256), 256), :]
            wat = pl.ds(pl.multiple_of(b * CW, CW), CW)
            acc[h, 0] += jnp.dot(xb, wg[wat, :], preferred_element_type=F32)
            acc[h, 1] += jnp.dot(xb, wu[wat, :], preferred_element_type=F32)
            v = xb.astype(F32) * ginv[:, pl.ds(pl.multiple_of(b * CW, 128), CW)]
            v = v * v
            ssq[h] += v[:, :128] + v[:, 128:256] + v[:, 256:]
            return c

        lax.fori_loop(0, len(offsets) * 2, body, 0)

    own_quarter(0, 0)
    spread(0, 0, 0)
    own_quarter(1, 0)
    own_quarter(1, 1)
    own_quarter(0, 1)
    spread(1, 0, 0)
    spread(1, 0, 1)
    spread(0, 0, 1)
    acc[...] = jnp.zeros_like(acc)
    ssq[...] = jnp.zeros_like(ssq)

    lo = [ab(h, -1, 0) for h in (0, 1)]
    hi = [ab(h, 1, 0) for h in (0, 1)]
    wait(0, 0, 0, 0, lo[0])
    send(0, 0, 0, 4, lo[0])
    spread(0, 1, 0)
    wait(0, 0, 0, 2, hi[0])
    spread(0, 2, 0)
    wait(1, 0, 0, 0, lo[1])
    send(1, 0, 0, 4, lo[1])
    wait(1, 0, 0, 3, hi[1])
    send(1, 0, 0, 5, hi[1])
    wait(0, 0, 0, 3, hi[0])
    send(0, 0, 0, 5, hi[0])
    spread(1, 1, 0)
    spread(1, 2, 1)
    spread(0, 2, 1)
    wait(0, 0, 0, 1, lo[0])
    spread(0, 1, 1)
    wait(1, 0, 0, 1, lo[1])
    spread(1, 1, 1)
    wait(1, 0, 0, 2, hi[1])
    spread(1, 2, 0)
    wcopies[0].wait()
    wcopies[1].wait()
    eat((0, 0))
    stage_f(0)
    for h in (0, 1):
        b = ab(h, 2, 0)
        wait(h, 0, 0, 4, b)
        spread(h, 3, 0)
        wait(h, 0, 0, 5, b)
        spread(h, 3, 1)
    eat((3, 0), (1, 0))
    stage_f(1)
    stage_w1(0)
    eat((2, 0), (0, 3), (0, 1))
    stage_f(2)
    stage_w1(1)
    eat((3, 3), (3, 1))
    stage_w2(0)
    eat((0, 2))
    stage_f(3)
    stage_w1(2)
    stage_w2(1)
    eat((1, 3), (1, 1), (3, 2))
    stage_w1(3)
    eat((2, 3), (2, 1))
    stage_w2(2)
    eat((1, 2))
    stage_w2(3)
    eat((2, 2))

    for h in (0, 1):
        total = jnp.sum(ssq[h], axis=1, keepdims=True)
        sc = lax.rsqrt(total / (16.0 * CW) + 1e-5)
        gate = acc[h, 0] * sc
        up = acc[h, 1] * sc
        hid[h] = (gate / (1.0 + jnp.exp(-gate)) * up).astype(BF16)
    wcopies[2].wait()

    def produce(i, blk, stage):
        todo = ((2,), (1, -1), (0,))[stage]
        for h in (0, 1):
            hv = hid[h]
            for d2 in todo:
                b = blk(h, i, d2)
                p2[b, h * 256 : (h + 1) * 256, :] = jnp.dot(
                    hv, wd[:, pl.ds(pl.multiple_of(b * CW, 128), CW)], preferred_element_type=F32
                ).astype(BF16)

    def back_copy(slot):
        p = slot // 2
        r = lax.rem(p, 2) * 2 + p // 2
        dst = lax.rem(gy + r, 4) * 2 + lax.rem(slot, 2)
        return rcopy(
            fin.at[pl.ds(pl.multiple_of(slot * 64, 64), 64)],
            ret.at[pl.ds(pl.multiple_of(g * 64, 64), 64)],
            rt_s.at[slot],
            rt_r.at[g],
            (dst, t),
        )

    def finish2(h, q, v):
        p = 2 * h + q
        fin[p * 128 : (p + 1) * 128, :] = v.astype(BF16)
        for c in (0, 1):
            slot = p * 2 + c
            if p == 0:

                @pl.when(gc != c)
                def _():
                    back_copy(slot).start()

                @pl.when(gc == c)
                def _():
                    ret[pl.ds(pl.multiple_of(g * 64, 64), 64), :] = fin[slot * 64 : slot * 64 + 64, :]

            else:
                back_copy(slot).start()

    sent2 = reduce_scatter(128, p2, rb2, y2, rc2, a2s, a2r, produce, finish2)

    def stat_wait(k, c):
        stat(k).wait_recv()
        return c

    lax.fori_loop(1, 16, stat_wait, 0)
    sums = jnp.sum(stat_in[...], axis=0)
    diff_all = sums[0:1, :] * lax.rsqrt(sums[1:2, :] / (16.0 * CW) + 1e-5)
    dcol = as_column(diff_all)
    wa = 1.0 / (1.0 + jnp.exp(-dcol))
    wb = 1.0 / (1.0 + jnp.exp(dcol))

    def ret_wait(k, c):
        e = lax.rem(g + k, 8)
        at = ret.at[pl.ds(pl.multiple_of(e * 64, 64), 64)]
        rcopy(at, at, rt_s.at[0], rt_r.at[e], (g, t)).wait_recv()
        return c

    lax.fori_loop(1, 8, ret_wait, 0)
    rv = ret[...]
    out_ref[...] = (
        rs[...].astype(F32)
        + wa * jnp.dot(back[0], rv, preferred_element_type=F32)
        + wb * jnp.dot(back[1], rv, preferred_element_type=F32)
    ).astype(BF16)

    for m in sent1 + ag_sent + sent2:
        m.wait_send()

    def stat_sent(k, c):
        stat(k).wait_send()
        return c

    def deal_sent(k, c):
        deal(k).wait_send()
        return c

    lax.fori_loop(1, 16, stat_sent, 0)
    lax.fori_loop(1, 8, deal_sent, 0)
    for slot in range(8):
        if slot < 2:

            @pl.when(gc != slot)
            def _():
                back_copy(slot).wait_send()

        else:
            back_copy(slot).wait_send()


def local(
    queries, new_kv, kv_cache, page_table, context_lengths, out_weight, residual_in,
    norm_gain, router_weight, routes, gate_weight, up_weight, down_weight,
):
    pool = kv_cache.shape[0] * kv_cache.shape[2]
    hb = pl.BlockSpec(memory_space=pl.ANY)
    dma = pltpu.SemaphoreType.DMA
    return pl.pallas_call(
        layer_kernel,
        out_shape=jax.ShapeDtypeStruct((128, CW), BF16),
        in_specs=[hb] * 13,
        out_specs=pl.BlockSpec(memory_space=pltpu.VMEM),
        scratch_shapes=[
            pltpu.VMEM((128, 256), BF16),
            pltpu.VMEM((128, 256), BF16),
            pltpu.VMEM((16, 128), jnp.int32),
            pltpu.VMEM((1, 128), jnp.int32),
            pltpu.VMEM((pool, 256), BF16),
            pltpu.VMEM((256, 16 * CW), BF16),
            pltpu.VMEM((128, CW), BF16),
            pltpu.VMEM((1, 16 * CW), F32),
            pltpu.VMEM((8, 16 * CW), BF16),
            pltpu.VMEM((2, 128), jnp.int32),
            pltpu.VMEM((pool // 16, 128), BF16),
            pltpu.VMEM((16, 128, CW), BF16),
            pltpu.VMEM((1, 16 * CW), F32),
            pltpu.VMEM((16 * CW, FW), BF16),
            pltpu.VMEM((16 * CW, FW), BF16),
            pltpu.VMEM((FW, 16 * CW), BF16),
            pltpu.VMEM((16, 512, CW), BF16),
            pltpu.VMEM((2, 2, 256, FW), F32),
            pltpu.VMEM((2, 256, 128), F32),
            pltpu.VMEM((2, 256, FW), BF16),
            pltpu.VMEM((16, 512, CW), BF16),
            pltpu.VMEM((2, 4, 3, 64, CW), BF16),
            pltpu.VMEM((2, 3, 64, CW), BF16),
            pltpu.VMEM((2, 3, 64, CW), BF16),
            pltpu.VMEM((2, 4, 6, 128, CW), BF16),
            pltpu.VMEM((2, 4, 256, CW), BF16),
            pltpu.VMEM((2, 6, 128, CW), BF16),
            pltpu.VMEM((128, CW), BF16),
            pltpu.VMEM((128, CW), BF16),
            pltpu.VMEM((8, 64, CW), BF16),
            pltpu.VMEM((512, CW), BF16),
            pltpu.VMEM((512, CW), BF16),
            pltpu.VMEM((8, 128), F32),
            pltpu.VMEM((16, 8, 128), F32),
            pltpu.VMEM((512, 128), BF16),
            pltpu.VMEM((2, 128, 512), BF16),
            dma((PARTS,)),
            dma((9,)),
            dma((3,)),
            dma((30,)),
            dma((30,)),
            dma((60,)),
            dma((60,)),
            dma((60,)),
            dma((60,)),
            dma((8,)),
            dma((8,)),
            dma((8,)),
            dma((8,)),
            dma((16,)),
            dma((16,)),
        ],
        compiler_params=pltpu.CompilerParams(
            collective_id=0, has_side_effects=True, vmem_limit_bytes=60 * 1024 * 1024
        ),
        cost_estimate=pl.CostEstimate(flops=11 << 30, bytes_accessed=26 << 20, transcendentals=1 << 21),
        name="layer",
    )(
        queries,
        new_kv.reshape(128, 256),
        page_table.T,
        context_lengths.reshape(1, 128),
        kv_cache.reshape(pool, 256),
        out_weight,
        residual_in,
        norm_gain.reshape(1, 16 * CW),
        router_weight.T,
        routes.T,
        gate_weight,
        up_weight,
        down_weight,
    )


def solution(mesh):
    return jax.shard_map(
        local,
        mesh=mesh,
        in_specs=(
            P("grp", "tp"),
            P("grp", "tp", None),
            P("grp", "tp", None, None),
            P("grp", None),
            P("grp"),
            P("tp", None),
            P("grp", "tp"),
            P(),
            P(),
            P("grp", None),
            P("grp", None, "tp"),
            P("grp", None, "tp"),
            P("grp", "tp", None),
        ),
        out_specs=P("grp", "tp"),
        check_vma=False,
    )
```

```python
import jax
import jax.numpy as jnp
from jax import lax
from jax.experimental import pallas as pl
from jax.experimental.pallas import tpu as pltpu
from jax.sharding import PartitionSpec as P

F32 = jnp.float32
BF16 = jnp.bfloat16
MESH = pl.DeviceIdType.MESH
NT = (((1,), (1,)), ((), ()))
TN = (((0,), (0,)), ((), ()))
PARTS = 5
NEG = -1e30
CW = 384
FW = 512
OFFS_OUT = (0, 3, 1, 2)
OFFS_IN = (2, 1, 3, 0)


def attend(q, own, live_ref, kv, kv_copies, part_rows):
    q2 = jnp.concatenate([q[:, :128], q[:, 128:]], axis=0)
    pages = part_rows // 16
    tok = lax.broadcasted_iota(jnp.int32, (256, 128), 0)
    offs = (tok & 15).astype(F32)
    tok16 = lax.broadcasted_iota(jnp.int32, (256, 16), 0) >> 4
    spread = (tok16 == lax.broadcasted_iota(jnp.int32, (256, 16), 1)).astype(F32).astype(BF16)
    s_own = lax.dot_general(own[:, :128], q2, NT, preferred_element_type=F32)
    row = lax.broadcasted_iota(jnp.int32, (128, 128), 0)
    col = lax.broadcasted_iota(jnp.int32, (128, 128), 1)
    eye = (row == col).astype(F32)
    eye = jnp.concatenate([eye, eye], axis=1)
    top = jnp.sum(s_own * eye, axis=0, keepdims=True)
    tot = jnp.ones((8, 256), F32) * 0.125
    own_v = jnp.transpose(own[:, 128:].astype(F32))
    acc = jnp.concatenate([own_v, own_v], axis=1)
    scale = 128.0 ** -0.5
    for i, copy in enumerate(kv_copies):
        copy.wait()
        tiles = []
        peak = top
        for c in range(part_rows // 256):
            at = i * part_rows + c * 256
            s = lax.dot_general(kv[at : at + 256, :128], q2, NT, preferred_element_type=F32)
            cn = live_ref[i * pages + c * 16 : i * pages + c * 16 + 16, :]
            m = offs < jnp.dot(spread, cn, preferred_element_type=F32)
            s = jnp.concatenate([jnp.where(m, s[:, :128], NEG), jnp.where(m, s[:, 128:], NEG)], axis=1)
            tiles.append(s)
            peak = jnp.maximum(peak, jnp.max(jnp.max(s.reshape(32, 8, 256), axis=0), axis=0, keepdims=True))
        fade = jnp.exp((top - peak) * scale)
        top = peak
        tot = tot * fade
        ps = []
        for s in tiles:
            p = jnp.exp((s - top) * scale)
            tot = tot + jnp.sum(p.reshape(32, 8, 256), axis=0)
            ps.append(p.astype(BF16))
        p = jnp.concatenate(ps, axis=0)
        acc = acc * fade + lax.dot_general(
            kv[i * part_rows : (i + 1) * part_rows, 128:], p, TN, preferred_element_type=F32
        )
    att = acc / jnp.sum(tot, axis=0, keepdims=True)
    return jnp.concatenate([jnp.transpose(att[:, :128]), jnp.transpose(att[:, 128:])], axis=1).astype(BF16)


def as_column(row):
    return jnp.transpose(jnp.broadcast_to(row, (128, 128)))[:, 0:1]


def route_maps(routes):
    lane = lax.broadcasted_iota(jnp.int32, (128, 128), 1)
    sub = lax.broadcasted_iota(jnp.int32, (128, 128), 0)
    hit0 = (sub == routes[0:1, :]).astype(F32)
    hit1 = (sub == routes[1:2, :]).astype(F32)
    hit = hit0 + hit1
    rank = jnp.dot(hit.astype(BF16), (sub < lane).astype(F32).astype(BF16), preferred_element_type=F32)
    spot = jnp.where(hit > 0.5, rank, -1.0)
    slot = lax.broadcasted_iota(jnp.int32, (64, 128), 0).astype(F32)
    place = jnp.concatenate([(slot == spot[e : e + 1, :]).astype(F32) for e in range(8)], axis=0)
    wide = lax.broadcasted_iota(jnp.int32, (128, 512), 1).astype(F32)

    def back(h, r):
        at = r.astype(F32) * 64.0 + jnp.sum(h * rank, axis=0, keepdims=True)
        return (wide == as_column(at)).astype(F32).astype(BF16)

    sign = hit0[:8, :] - hit1[:8, :]
    return place.astype(BF16), back(hit0, routes[0:1, :]), back(hit1, routes[1:2, :]), sign


def layer_kernel(
    q_hbm, own_hbm, pt_hbm, len_hbm, kv_hbm, w_hbm, res_hbm, gain_hbm, router_hbm, routes_hbm, wg_hbm, wu_hbm, wd_hbm,
    out_ref,
    q_ref, own_ref, pt_ref, len_ref, kv, w, res_ref, gain_ref, router_ref, routes_ref, live, part, ginv,
    wg, wu, wd, xg, acc, ssq, hid, p2, rb1, y1, rc1, rb2, y2, rc2,
    rs, xs, ds, ret, stat_out, stat_in, place, back,
    ksem, msem, wsem, a1s, a1r, ags, agr, a2s, a2r, ds_s, ds_r, rt_s, rt_r, st_s, st_r,
):
    g = lax.axis_index("grp")
    t = lax.axis_index("tp")
    gy, gc = g // 2, lax.rem(g, 2)
    tz, tx = t // 4, lax.rem(t, 4)
    me = ((tx, tz), (tz, tx))

    def tid(h, c1, c2):
        return c2 * 4 + c1 if h == 0 else c1 * 4 + c2

    def m4(v):
        return lax.rem(v + 4, 4)

    barrier = pltpu.get_barrier_semaphore()

    def greet_t(k, c):
        pl.semaphore_signal(barrier, inc=1, device_id=(g, lax.rem(t + k, 16)), device_id_type=MESH)
        return c

    def greet_g(k, c):
        pl.semaphore_signal(barrier, inc=1, device_id=(lax.rem(g + k, 8), t), device_id_type=MESH)
        return c

    around = (
        tz * 4 + m4(tx + 1), tz * 4 + m4(tx - 1), m4(tz + 1) * 4 + tx, m4(tz - 1) * 4 + tx,
    )

    def greet_a(k, c):
        for a in around:
            pl.semaphore_signal(barrier, inc=1, device_id=(lax.rem(g + k, 8), a), device_id_type=MESH)
        return c

    lax.fori_loop(1, 16, greet_t, 0)
    lax.fori_loop(1, 8, greet_a, 0)
    lax.fori_loop(1, 8, greet_g, 0)

    step = kv.shape[0] // PARTS
    small = [
        pltpu.make_async_copy(src, dst, msem.at[i])
        for i, (src, dst) in enumerate(
            (
                (pt_hbm, pt_ref), (len_hbm, len_ref), (q_hbm, q_ref), (own_hbm, own_ref), (routes_hbm, routes_ref),
                (res_hbm, res_ref), (gain_hbm, gain_ref), (router_hbm, router_ref), (w_hbm, w),
            )
        )
    ]
    kv_copies = [
        pltpu.make_async_copy(kv_hbm.at[pl.ds(i * step, step)], kv.at[pl.ds(i * step, step)], ksem.at[i])
        for i in range(PARTS)
    ]
    wcopies = [
        pltpu.make_async_copy(src.at[0], dst, wsem.at[i])
        for i, (src, dst) in enumerate(((wg_hbm, wg), (wu_hbm, wu), (wd_hbm, wd)))
    ]
    for c in small[:5] + kv_copies + small[5:] + wcopies:
        c.start()

    small[0].wait()
    small[1].wait()
    pages = live.shape[0]
    page_ids = lax.broadcasted_iota(jnp.int32, (pages, 128), 0)
    lens = len_ref[...]
    count = jnp.zeros((pages, 128), jnp.int32)
    for j in range(16):
        here = jnp.clip(lens - 16 * j, 0, 16)
        count = count + jnp.where(page_ids == pt_ref[j : j + 1, :], here, 0)
    live[...] = count.astype(F32).astype(BF16)
    small[2].wait()
    small[3].wait()
    attn = attend(q_ref[...], own_ref[...], live, kv, kv_copies, step)
    small[8].wait()

    pl.semaphore_wait(barrier, 50)

    def rcopy(src, dst, ss, rr, dev):
        return pltpu.make_async_remote_copy(
            src_ref=src, dst_ref=dst, send_sem=ss, recv_sem=rr, device_id=dev, device_id_type=MESH
        )

    def reduce_scatter(rows, src, rb, y, rc, ss, rr, produce, last):
        def q_rows(h, q):
            return pl.ds((2 * h + q) * rows, rows)

        def nbr(h, axis, d):
            c = list(me[h])
            c[axis] = m4(c[axis] + d)
            return (g, tid(h, c[0], c[1]))

        def blk(h, i, d2):
            return tid(h, m4(me[h][0] + OFFS_IN[i]), m4(me[h][1] + d2))

        def msg1(h, i, k, from_buf=None):
            d2, q, d = ((2, 0, 1), (2, 1, -1), (1, 1, 1), (-1, 0, -1), (1, 0, 1), (-1, 1, -1))[k]
            s = src.at[blk(h, i, d2), q_rows(h, q)] if from_buf is None else rb.at[h, i, from_buf]
            n = h * 24 + i * 6 + k
            return rcopy(s, rb.at[h, i, k], ss.at[n], rr.at[n], nbr(h, 1, d))

        def msg2(h, k, i, from_buf=None):
            q, d = ((0, 1), (1, -1), (1, 1), (0, -1), (0, 1), (1, -1))[k]
            s = y.at[h, i, pl.ds(q * rows, rows)] if from_buf is None else rc.at[h, from_buf]
            n = 48 + h * 6 + k
            return rcopy(s, rc.at[h, k], ss.at[n], rr.at[n], nbr(h, 0, d))

        sent = []

        def go(m):
            m.start()
            sent.append(m)

        def rows_of(ref, h, q):
            return lambda c: ref.at[pl.ds((2 * h + q) * rows + c * 64, 64)]

        def halves(ref):
            return lambda c: ref.at[pl.ds(c * 64, 64)]

        def end(h, q, term, part_of, axis, d):
            for c in (0, 1):
                go(last(h, q, c, term, part_of(c), nbr(h, axis, d)[1]))

        def stage_g(i):
            produce(i, blk, 0)
            for h in (0, 1):
                go(msg1(h, i, 0))
                go(msg1(h, i, 1))
            produce(i, blk, 1)
            for h in (0, 1):
                if i < 3:
                    go(msg1(h, i, 2))
                    go(msg1(h, i, 3))
                else:
                    end(h, 1, 1, rows_of(src.at[blk(h, 3, 1)], h, 1), 1, 1)
                    end(h, 0, 2, rows_of(src.at[blk(h, 3, -1)], h, 0), 1, -1)

        def stage_h(i):
            for h in (0, 1):
                msg1(h, i, 0).wait_recv()
                rb[h, i, 0] = (
                    rb[h, i, 0].astype(F32) + src[blk(h, i, 1), q_rows(h, 0)].astype(F32)
                ).astype(BF16)
                if i < 3:
                    go(msg1(h, i, 4, 0))
                else:
                    end(h, 0, 1, halves(rb.at[h, i, 0]), 1, 1)
                msg1(h, i, 1).wait_recv()
                rb[h, i, 1] = (
                    rb[h, i, 1].astype(F32) + src[blk(h, i, -1), q_rows(h, 1)].astype(F32)
                ).astype(BF16)
                if i < 3:
                    go(msg1(h, i, 5, 1))
                else:
                    end(h, 1, 2, halves(rb.at[h, i, 1]), 1, -1)

        def stage_j(i):
            produce(i, blk, 2)
            for h in (0, 1):
                for q, (k1, k2) in ((0, (3, 4)), (1, (2, 5))):
                    msg1(h, i, k1).wait_recv()
                    msg1(h, i, k2).wait_recv()
                    y[h, i, pl.ds(q * rows, rows)] = (
                        src[blk(h, i, 0), q_rows(h, q)].astype(F32)
                        + rb[h, i, k1].astype(F32)
                        + rb[h, i, k2].astype(F32)
                    ).astype(BF16)
                    if i == 0:
                        go(msg2(h, q, 0))
                if i == 1:
                    end(h, 1, 3, lambda c: y.at[h, 1, pl.ds(rows + c * 64, 64)], 0, 1)
                    msg2(h, 0, 1).wait_recv()
                    rc[h, 0] = (rc[h, 0].astype(F32) + y[h, 1, pl.ds(0, rows)].astype(F32)).astype(BF16)
                    end(h, 0, 3, halves(rc.at[h, 0]), 0, 1)
                if i == 2:
                    end(h, 0, 4, lambda c: y.at[h, 2, pl.ds(c * 64, 64)], 0, -1)
                    msg2(h, 1, 2).wait_recv()
                    rc[h, 1] = (rc[h, 1].astype(F32) + y[h, 2, pl.ds(rows, rows)].astype(F32)).astype(BF16)
                    end(h, 1, 4, halves(rc.at[h, 1]), 0, -1)

        stage_g(0)
        stage_g(1)
        stage_h(0)
        stage_g(2)
        stage_h(1)
        stage_j(0)
        stage_g(3)
        produce(3, blk, 2)
        own_terms(sent)
        stage_h(2)
        stage_j(1)
        stage_h(3)
        stage_j(2)
        return sent

    sent1 = []

    def project(n, c):
        def third(v):
            return v + (v == 2).astype(jnp.int32)

        m = n - 7
        ox = jnp.where(n < 4, 2, jnp.where(n < 7, third(n - 4), third(m // 3)))
        oz = jnp.where(n < 4, n, jnp.where(n < 7, 2, third(lax.rem(m, 3))))
        b = m4(tz + oz) * 4 + m4(tx + ox)
        part[b] = jnp.dot(
            attn, w[:, pl.ds(pl.multiple_of(b * CW, 128), CW)], preferred_element_type=F32
        ).astype(BF16)
        return c

    def far(h, axis, o):
        c = list(me[h])
        c[axis] = m4(c[axis] + o)
        return (g, tid(h, c[0], c[1]))

    def out1(h, i, k):
        o1, o2 = OFFS_IN[i], (2, 1, -1)[k]
        n = h * 12 + i * 3 + k
        return rcopy(
            part.at[tid(h, m4(me[h][0] + o1), m4(me[h][1] + o2)), pl.ds(h * 64, 64)],
            rb1.at[h, i, k], a1s.at[n], a1r.at[n], far(h, 1, o2),
        )

    def out2(h, i):
        n = 24 + h * 3 + i
        return rcopy(y1.at[h, i], rc1.at[h, i], a1s.at[n], a1r.at[n], far(h, 0, OFFS_IN[i]))

    def go1(m):
        m.start()
        sent1.append(m)

    lax.fori_loop(0, 7, project, 0)
    for k in range(3):
        for h in (0, 1):
            go1(out1(h, 0, k))
    lax.fori_loop(7, 16, project, 0)
    for i in (1, 2, 3):
        for k in range(3):
            for h in (0, 1):
                go1(out1(h, i, k))
    small[4].wait()
    pl_m, b0, b1, sign = route_maps(routes_ref[...])
    place[...] = pl_m
    back[0] = b0
    back[1] = b1
    for c in small[5:8]:
        c.wait()
    ginv[...] = 1.0 / gain_ref[...]
    gain_row = gain_ref[:, pl.ds(pl.multiple_of(t * CW, 128), CW)]
    for i in range(4):
        for h in (0, 1):
            for k in range(3):
                out1(h, i, k).wait_recv()
            v = part[tid(h, m4(me[h][0] + OFFS_IN[i]), me[h][1]), h * 64 : h * 64 + 64, :].astype(F32)
            for k in range(3):
                v = v + rb1[h, i, k].astype(F32)
            if i < 3:
                y1[h, i] = v.astype(BF16)
                go1(out2(h, i))
            else:
                for k in range(3):
                    out2(h, k).wait_recv()
                    v = v + rc1[h, k].astype(F32)
                at = pl.ds(h * 64, 64)
                r = (res_ref[at, :].astype(F32) + v).astype(BF16)
                rs[at, :] = r
                xs[at, :] = (r.astype(F32) * gain_row).astype(BF16)

    x = xs[...]
    ds[...] = jnp.dot(place[...], x, preferred_element_type=F32).astype(BF16).reshape(8, 64, CW)

    def seat(src_y, src_c, dst_y):
        r = m4(src_y - dst_y)
        p = lax.rem(r, 2) * 2 + r // 2
        return pl.multiple_of(p * 128 + src_c * 64, 64), p * 2 + src_c

    own_row, own_slot = seat(gy, gc, gy)
    xg[t, pl.ds(own_row, 64), :] = ds[g]

    def deal(k):
        e = lax.rem(g + k, 8)
        row, slot = seat(gy, gc, e // 2)
        return rcopy(ds.at[e], xg.at[t, pl.ds(row, 64)], ds_s.at[k], ds_r.at[slot], (e, t))

    def deal_start(k, c):
        deal(k).start()
        return c

    lax.fori_loop(1, 8, deal_start, 0)

    def dealt(slot):
        at = xg.at[t, pl.ds(pl.multiple_of(slot * 64, 64), 64)]
        return rcopy(at, at, ds_s.at[0], ds_r.at[slot], (g, t))

    logit = lax.dot_general(
        router_ref[:, pl.ds(pl.multiple_of(t * CW, 128), CW)], x, NT, preferred_element_type=F32
    )
    diff = jnp.sum(logit * sign, axis=0, keepdims=True)
    r32 = rs[...].astype(F32)
    sq = jnp.sum(r32 * r32, axis=1, keepdims=True)
    sq = jnp.transpose(jnp.broadcast_to(sq, (128, 128)))[:8, :]
    sub8 = lax.broadcasted_iota(jnp.int32, (8, 128), 0)
    tile = jnp.where(sub8 == 0, diff, jnp.where(sub8 == 1, sq, 0.0))
    stat_out[...] = tile
    stat_in[0] = tile

    def stat(k):
        return rcopy(stat_out, stat_in.at[k], st_s.at[k], st_r.at[k], (g, lax.rem(t + k, 16)))

    def stat_start(k, c):
        stat(k).start()
        return c

    lax.fori_loop(1, 16, stat_start, 0)

    ag_sent = []

    def ag(h, phase, i, k, b):
        q, d = ((0, 1), (1, 1), (0, -1), (1, -1), (0, 1), (1, -1))[k]
        c = list(me[h])
        c[phase] = m4(c[phase] + d)
        ref = xg.at[b, pl.ds((2 * h + q) * 128, 128)]
        n = h * 30 + phase * 6 + i * 6 + k
        return rcopy(ref, ref, ags.at[n], agr.at[n], (g, tid(h, c[0], c[1])))

    def send(*a):
        m = ag(*a)
        m.start()
        ag_sent.append(m)

    def ab(h, o1, o2):
        return tid(h, m4(me[h][0] + o1), m4(me[h][1] + o2))

    def wait(h, phase, i, k, b):
        ag(h, phase, i, k, b).wait_recv()

    def spread(h, i, q):
        b = ab(h, OFFS_OUT[i], 0)
        send(h, 1, i, q, b)
        send(h, 1, i, 2 + q, b)

    def own_quarter(h, q):
        p = 2 * h + q
        for c in (0, 1):
            slot = p * 2 + c
            if p == 0:

                @pl.when(gc != c)
                def _():
                    dealt(slot).wait_recv()

            else:
                dealt(slot).wait_recv()
        send(h, 0, 0, q, t)
        send(h, 0, 0, 2 + q, t)

    def stage_f(i):
        for h in (0, 1):
            b = ab(h, OFFS_OUT[i], -1)
            wait(h, 1, i, 0, b)
            send(h, 1, i, 4, b)
            b = ab(h, OFFS_OUT[i], 1)
            wait(h, 1, i, 3, b)
            send(h, 1, i, 5, b)

    def stage_w1(i):
        for h in (0, 1):
            wait(h, 1, i, 1, ab(h, OFFS_OUT[i], -1))
            wait(h, 1, i, 2, ab(h, OFFS_OUT[i], 1))

    def stage_w2(i):
        for h in (0, 1):
            b = ab(h, OFFS_OUT[i], 2)
            wait(h, 1, i, 4, b)
            wait(h, 1, i, 5, b)

    def eat(*offsets):
        def body(n, c):
            h = lax.rem(n, 2)
            j = n // 2
            o1, o2 = offsets[0]
            for m, (u1, u2) in enumerate(offsets):
                o1 = jnp.where(j == m, u1, o1)
                o2 = jnp.where(j == m, u2, o2)
            c1 = m4(jnp.where(h == 0, tx, tz) + o1)
            c2 = m4(jnp.where(h == 0, tz, tx) + o2)
            b = jnp.where(h == 0, c2 * 4 + c1, c1 * 4 + c2)
            xb = xg[b, pl.ds(pl.multiple_of(h * 256, 256), 256), :]
            wat = pl.ds(pl.multiple_of(b * CW, CW), CW)
            acc[h, 0] += jnp.dot(xb, wg[wat, :], preferred_element_type=F32)
            acc[h, 1] += jnp.dot(xb, wu[wat, :], preferred_element_type=F32)
            v = xb.astype(F32) * ginv[:, pl.ds(pl.multiple_of(b * CW, 128), CW)]
            v = v * v
            ssq[h] += v[:, :128] + v[:, 128:256] + v[:, 256:]
            return c

        lax.fori_loop(0, len(offsets) * 2, body, 0)

    own_quarter(0, 0)
    spread(0, 0, 0)
    own_quarter(1, 0)
    own_quarter(1, 1)
    own_quarter(0, 1)
    spread(1, 0, 0)
    spread(1, 0, 1)
    spread(0, 0, 1)
    acc[...] = jnp.zeros_like(acc)
    ssq[...] = jnp.zeros_like(ssq)

    lo = [ab(h, -1, 0) for h in (0, 1)]
    hi = [ab(h, 1, 0) for h in (0, 1)]
    wait(0, 0, 0, 0, lo[0])
    send(0, 0, 0, 4, lo[0])
    spread(0, 1, 0)
    wait(0, 0, 0, 2, hi[0])
    spread(0, 2, 0)
    wait(1, 0, 0, 0, lo[1])
    send(1, 0, 0, 4, lo[1])
    wait(1, 0, 0, 3, hi[1])
    send(1, 0, 0, 5, hi[1])
    wait(0, 0, 0, 3, hi[0])
    send(0, 0, 0, 5, hi[0])
    spread(1, 1, 0)
    spread(1, 2, 1)
    spread(0, 2, 1)
    wait(0, 0, 0, 1, lo[0])
    spread(0, 1, 1)
    wait(1, 0, 0, 1, lo[1])
    spread(1, 1, 1)
    wait(1, 0, 0, 2, hi[1])
    spread(1, 2, 0)
    wcopies[0].wait()
    wcopies[1].wait()
    eat((0, 0))
    stage_f(0)
    for h in (0, 1):
        b = ab(h, 2, 0)
        wait(h, 0, 0, 4, b)
        spread(h, 3, 0)
        wait(h, 0, 0, 5, b)
        spread(h, 3, 1)
    eat((3, 0), (1, 0))
    stage_f(1)
    stage_w1(0)
    eat((2, 0), (0, 3), (0, 1))
    stage_f(2)
    stage_w1(1)
    eat((3, 3), (3, 1))
    stage_w2(0)
    eat((0, 2))
    stage_f(3)
    stage_w1(2)
    stage_w2(1)
    eat((1, 3), (1, 1), (3, 2))
    stage_w1(3)
    eat((2, 3), (2, 1))
    stage_w2(2)
    eat((1, 2))
    stage_w2(3)
    eat((2, 2))

    for h in (0, 1):
        total = jnp.sum(ssq[h], axis=1, keepdims=True)
        sc = lax.rsqrt(total / (16.0 * CW) + 1e-5)
        gate = acc[h, 0] * sc
        up = acc[h, 1] * sc
        hid[h] = (gate / (1.0 + jnp.exp(-gate)) * up).astype(BF16)
    wcopies[2].wait()

    def produce(i, blk, stage):
        todo = ((2,), (1, -1), (0,))[stage]
        for h in (0, 1):
            hv = hid[h]
            for d2 in todo:
                b = blk(h, i, d2)
                p2[b, h * 256 : (h + 1) * 256, :] = jnp.dot(
                    hv, wd[:, pl.ds(pl.multiple_of(b * CW, 128), CW)], preferred_element_type=F32
                ).astype(BF16)

    def home(h, q, c):
        r = (0, 2, 1, 3)[2 * h + q]
        return lax.rem(gy + r, 4) * 2 + c

    def last(h, q, c, term, src, to):
        n = ((2 * h + q) * 2 + c) * 5 + term
        return rcopy(
            src, ret.at[term, pl.ds(pl.multiple_of(g * 64, 64), 64)],
            rt_s.at[n], rt_r.at[term * 8 + g], (home(h, q, c), to),
        )

    def own_term(h, q, c):
        return last(h, q, c, 0, p2.at[t, pl.ds((2 * h + q) * 128 + c * 64, 64)], t)

    def own_terms(sent):
        for h in (0, 1):
            for q in (0, 1):
                for c in (0, 1):
                    if h == 0 and q == 0:

                        @pl.when(gc != c)
                        def _():
                            own_term(0, 0, c).start()

                        @pl.when(gc == c)
                        def _():
                            ret[0, pl.ds(pl.multiple_of(g * 64, 64), 64), :] = p2[t, c * 64 : c * 64 + 64, :]

                    else:
                        m = own_term(h, q, c)
                        m.start()
                        sent.append(m)

    sent2 = reduce_scatter(128, p2, rb2, y2, rc2, a2s, a2r, produce, last)

    def stat_wait(k, c):
        stat(k).wait_recv()
        return c

    lax.fori_loop(1, 16, stat_wait, 0)
    sums = jnp.sum(stat_in[...], axis=0)
    diff_all = sums[0:1, :] * lax.rsqrt(sums[1:2, :] / (16.0 * CW) + 1e-5)
    dcol = as_column(diff_all)
    wa = 1.0 / (1.0 + jnp.exp(-dcol))
    wb = 1.0 / (1.0 + jnp.exp(dcol))

    def term_wait(term, e):
        at = ret.at[term, pl.ds(pl.multiple_of(e * 64, 64), 64)]
        rcopy(at, at, rt_s.at[0], rt_r.at[term * 8 + e], (g, t)).wait_recv()

    def ret_wait(k, c):
        term_wait(0, lax.rem(g + k, 8))
        return c

    def rest_wait(e, c):
        for term in (3, 1, 2, 4):
            term_wait(term, e)
        return c

    lax.fori_loop(1, 8, ret_wait, 0)
    lax.fori_loop(0, 8, rest_wait, 0)
    rv = ret[0].astype(F32)
    for term in (1, 2, 3, 4):
        rv = rv + ret[term].astype(F32)
    rv = rv.astype(BF16)
    out_ref[...] = (
        rs[...].astype(F32)
        + wa * jnp.dot(back[0], rv, preferred_element_type=F32)
        + wb * jnp.dot(back[1], rv, preferred_element_type=F32)
    ).astype(BF16)

    for m in sent1 + ag_sent + sent2:
        m.wait_send()

    def stat_sent(k, c):
        stat(k).wait_send()
        return c

    def deal_sent(k, c):
        deal(k).wait_send()
        return c

    lax.fori_loop(1, 16, stat_sent, 0)
    lax.fori_loop(1, 8, deal_sent, 0)
    for c in (0, 1):

        @pl.when(gc != c)
        def _():
            own_term(0, 0, c).wait_send()


def local(
    queries, new_kv, kv_cache, page_table, context_lengths, out_weight, residual_in,
    norm_gain, router_weight, routes, gate_weight, up_weight, down_weight,
):
    pool = kv_cache.shape[0] * kv_cache.shape[2]
    hb = pl.BlockSpec(memory_space=pl.ANY)
    dma = pltpu.SemaphoreType.DMA
    return pl.pallas_call(
        layer_kernel,
        out_shape=jax.ShapeDtypeStruct((128, CW), BF16),
        in_specs=[hb] * 13,
        out_specs=pl.BlockSpec(memory_space=pltpu.VMEM),
        scratch_shapes=[
            pltpu.VMEM((128, 256), BF16),
            pltpu.VMEM((128, 256), BF16),
            pltpu.VMEM((16, 128), jnp.int32),
            pltpu.VMEM((1, 128), jnp.int32),
            pltpu.VMEM((pool, 256), BF16),
            pltpu.VMEM((256, 16 * CW), BF16),
            pltpu.VMEM((128, CW), BF16),
            pltpu.VMEM((1, 16 * CW), F32),
            pltpu.VMEM((8, 16 * CW), BF16),
            pltpu.VMEM((2, 128), jnp.int32),
            pltpu.VMEM((pool // 16, 128), BF16),
            pltpu.VMEM((16, 128, CW), BF16),
            pltpu.VMEM((1, 16 * CW), F32),
            pltpu.VMEM((16 * CW, FW), BF16),
            pltpu.VMEM((16 * CW, FW), BF16),
            pltpu.VMEM((FW, 16 * CW), BF16),
            pltpu.VMEM((16, 512, CW), BF16),
            pltpu.VMEM((2, 2, 256, FW), F32),
            pltpu.VMEM((2, 256, 128), F32),
            pltpu.VMEM((2, 256, FW), BF16),
            pltpu.VMEM((16, 512, CW), BF16),
            pltpu.VMEM((2, 4, 3, 64, CW), BF16),
            pltpu.VMEM((2, 3, 64, CW), BF16),
            pltpu.VMEM((2, 3, 64, CW), BF16),
            pltpu.VMEM((2, 4, 6, 128, CW), BF16),
            pltpu.VMEM((2, 4, 256, CW), BF16),
            pltpu.VMEM((2, 6, 128, CW), BF16),
            pltpu.VMEM((128, CW), BF16),
            pltpu.VMEM((128, CW), BF16),
            pltpu.VMEM((8, 64, CW), BF16),
            pltpu.VMEM((5, 512, CW), BF16),
            pltpu.VMEM((8, 128), F32),
            pltpu.VMEM((16, 8, 128), F32),
            pltpu.VMEM((512, 128), BF16),
            pltpu.VMEM((2, 128, 512), BF16),
            dma((PARTS,)),
            dma((9,)),
            dma((3,)),
            dma((30,)),
            dma((30,)),
            dma((60,)),
            dma((60,)),
            dma((60,)),
            dma((60,)),
            dma((8,)),
            dma((8,)),
            dma((40,)),
            dma((40,)),
            dma((16,)),
            dma((16,)),
        ],
        compiler_params=pltpu.CompilerParams(
            collective_id=0, has_side_effects=True, vmem_limit_bytes=60 * 1024 * 1024
        ),
        cost_estimate=pl.CostEstimate(flops=11 << 30, bytes_accessed=26 << 20, transcendentals=1 << 21),
        name="layer",
    )(
        queries,
        new_kv.reshape(128, 256),
        page_table.T,
        context_lengths.reshape(1, 128),
        kv_cache.reshape(pool, 256),
        out_weight,
        residual_in,
        norm_gain.reshape(1, 16 * CW),
        router_weight.T,
        routes.T,
        gate_weight,
        up_weight,
        down_weight,
    )


def solution(mesh):
    return jax.shard_map(
        local,
        mesh=mesh,
        in_specs=(
            P("grp", "tp"),
            P("grp", "tp", None),
            P("grp", "tp", None, None),
            P("grp", None),
            P("grp"),
            P("tp", None),
            P("grp", "tp"),
            P(),
            P(),
            P("grp", None),
            P("grp", None, "tp"),
            P("grp", None, "tp"),
            P("grp", "tp", None),
        ),
        out_specs=P("grp", "tp"),
        check_vma=False,
    )
```

```python
import jax
import jax.numpy as jnp
from jax import lax
from jax.experimental import pallas as pl
from jax.experimental.pallas import tpu as pltpu
from jax.sharding import PartitionSpec as P

F32 = jnp.float32
BF16 = jnp.bfloat16
MESH = pl.DeviceIdType.MESH
NT = (((1,), (1,)), ((), ()))
TN = (((0,), (0,)), ((), ()))
PARTS = 5
NEG = -1e30
CW = 384
FW = 512
OFFS_OUT = (0, 3, 1, 2)
OFFS_IN = (2, 1, 3, 0)


def attend(q, own, live_ref, kv, kv_copies, part_rows):
    q2 = jnp.concatenate([q[:, :128], q[:, 128:]], axis=0)
    pages = part_rows // 16
    tok = lax.broadcasted_iota(jnp.int32, (256, 128), 0)
    offs = (tok & 15).astype(F32)
    tok16 = lax.broadcasted_iota(jnp.int32, (256, 16), 0) >> 4
    spread = (tok16 == lax.broadcasted_iota(jnp.int32, (256, 16), 1)).astype(F32).astype(BF16)
    s_own = lax.dot_general(own[:, :128], q2, NT, preferred_element_type=F32)
    row = lax.broadcasted_iota(jnp.int32, (128, 128), 0)
    col = lax.broadcasted_iota(jnp.int32, (128, 128), 1)
    eye = (row == col).astype(F32)
    eye = jnp.concatenate([eye, eye], axis=1)
    top = jnp.sum(s_own * eye, axis=0, keepdims=True)
    tot = jnp.ones((8, 256), F32) * 0.125
    own_v = jnp.transpose(own[:, 128:].astype(F32))
    acc = jnp.concatenate([own_v, own_v], axis=1)
    scale = 128.0 ** -0.5
    for i, copy in enumerate(kv_copies):
        copy.wait()
        tiles = []
        peak = top
        for c in range(part_rows // 256):
            at = i * part_rows + c * 256
            s = lax.dot_general(kv[at : at + 256, :128], q2, NT, preferred_element_type=F32)
            cn = live_ref[i * pages + c * 16 : i * pages + c * 16 + 16, :]
            m = offs < jnp.dot(spread, cn, preferred_element_type=F32)
            s = jnp.concatenate([jnp.where(m, s[:, :128], NEG), jnp.where(m, s[:, 128:], NEG)], axis=1)
            tiles.append(s)
            peak = jnp.maximum(peak, jnp.max(jnp.max(s.reshape(32, 8, 256), axis=0), axis=0, keepdims=True))
        fade = jnp.exp((top - peak) * scale)
        top = peak
        tot = tot * fade
        ps = []
        for s in tiles:
            p = jnp.exp((s - top) * scale)
            tot = tot + jnp.sum(p.reshape(32, 8, 256), axis=0)
            ps.append(p.astype(BF16))
        p = jnp.concatenate(ps, axis=0)
        acc = acc * fade + lax.dot_general(
            kv[i * part_rows : (i + 1) * part_rows, 128:], p, TN, preferred_element_type=F32
        )
    att = acc / jnp.sum(tot, axis=0, keepdims=True)
    return jnp.concatenate([jnp.transpose(att[:, :128]), jnp.transpose(att[:, 128:])], axis=1).astype(BF16)


def as_column(row):
    return jnp.transpose(jnp.broadcast_to(row, (128, 128)))[:, 0:1]


def route_maps(routes):
    lane = lax.broadcasted_iota(jnp.int32, (128, 128), 1)
    sub = lax.broadcasted_iota(jnp.int32, (128, 128), 0)
    hit0 = (sub == routes[0:1, :]).astype(F32)
    hit1 = (sub == routes[1:2, :]).astype(F32)
    hit = hit0 + hit1
    rank = jnp.dot(hit.astype(BF16), (sub < lane).astype(F32).astype(BF16), preferred_element_type=F32)
    spot = jnp.where(hit > 0.5, rank, -1.0)
    slot = lax.broadcasted_iota(jnp.int32, (64, 128), 0).astype(F32)
    place = jnp.concatenate([(slot == spot[e : e + 1, :]).astype(F32) for e in range(8)], axis=0)
    wide = lax.broadcasted_iota(jnp.int32, (128, 512), 1).astype(F32)

    def back(h, r):
        at = r.astype(F32) * 64.0 + jnp.sum(h * rank, axis=0, keepdims=True)
        return (wide == as_column(at)).astype(F32).astype(BF16)

    sign = hit0[:8, :] - hit1[:8, :]
    return place.astype(BF16), back(hit0, routes[0:1, :]), back(hit1, routes[1:2, :]), sign


def layer_kernel(
    q_hbm, own_hbm, pt_hbm, len_hbm, kv_hbm, w_hbm, res_hbm, gain_hbm, router_hbm, routes_hbm, wg_hbm, wu_hbm, wd_hbm,
    out_ref,
    q_ref, own_ref, pt_ref, len_ref, kv, w, res_ref, gain_ref, router_ref, routes_ref, live, part, ginv,
    wg, wu, wd, xg, acc, ssq, hid, p2, rb1, y1, rc1, rb2, y2, rc2,
    rs, xs, ds, fin, ret, stat_out, stat_in, place, back,
    ksem, msem, wsem, a1s, a1r, ags, agr, a2s, a2r, ds_s, ds_r, ea_s, ea_r, rt_s, rt_r, st_s, st_r,
):
    g = lax.axis_index("grp")
    t = lax.axis_index("tp")
    gy, gc = g // 2, lax.rem(g, 2)
    tz, tx = t // 4, lax.rem(t, 4)
    me = ((tx, tz), (tz, tx))

    def tid(h, c1, c2):
        return c2 * 4 + c1 if h == 0 else c1 * 4 + c2

    def m4(v):
        return lax.rem(v + 4, 4)

    barrier = pltpu.get_barrier_semaphore()

    def greet_t(k, c):
        pl.semaphore_signal(barrier, inc=1, device_id=(g, lax.rem(t + k, 16)), device_id_type=MESH)
        return c

    def greet_g(k, c):
        pl.semaphore_signal(barrier, inc=1, device_id=(lax.rem(g + k, 8), t), device_id_type=MESH)
        return c

    around = (
        tz * 4 + m4(tx + 1), tz * 4 + m4(tx - 1), m4(tz + 1) * 4 + tx, m4(tz - 1) * 4 + tx,
    )
    for a in around:
        pl.semaphore_signal(barrier, inc=1, device_id=(gy * 2 + 1 - gc, a), device_id_type=MESH)
    lax.fori_loop(1, 16, greet_t, 0)
    lax.fori_loop(1, 8, greet_g, 0)

    step = kv.shape[0] // PARTS
    small = [
        pltpu.make_async_copy(src, dst, msem.at[i])
        for i, (src, dst) in enumerate(
            (
                (pt_hbm, pt_ref), (len_hbm, len_ref), (q_hbm, q_ref), (own_hbm, own_ref), (routes_hbm, routes_ref),
                (res_hbm, res_ref), (gain_hbm, gain_ref), (router_hbm, router_ref), (w_hbm, w),
            )
        )
    ]
    kv_copies = [
        pltpu.make_async_copy(kv_hbm.at[pl.ds(i * step, step)], kv.at[pl.ds(i * step, step)], ksem.at[i])
        for i in range(PARTS)
    ]
    wcopies = [
        pltpu.make_async_copy(src.at[0], dst, wsem.at[i])
        for i, (src, dst) in enumerate(((wg_hbm, wg), (wu_hbm, wu), (wd_hbm, wd)))
    ]
    for c in small[:5] + kv_copies + small[5:] + wcopies:
        c.start()

    small[0].wait()
    small[1].wait()
    pages = live.shape[0]
    page_ids = lax.broadcasted_iota(jnp.int32, (pages, 128), 0)
    lens = len_ref[...]
    count = jnp.zeros((pages, 128), jnp.int32)
    for j in range(16):
        here = jnp.clip(lens - 16 * j, 0, 16)
        count = count + jnp.where(page_ids == pt_ref[j : j + 1, :], here, 0)
    live[...] = count.astype(F32).astype(BF16)
    small[2].wait()
    small[3].wait()
    attn = attend(q_ref[...], own_ref[...], live, kv, kv_copies, step)
    small[8].wait()

    pl.semaphore_wait(barrier, 26)

    def rcopy(src, dst, ss, rr, dev):
        return pltpu.make_async_remote_copy(
            src_ref=src, dst_ref=dst, send_sem=ss, recv_sem=rr, device_id=dev, device_id_type=MESH
        )

    def reduce_scatter(rows, src, rb, y, rc, ss, rr, produce, finish):
        def q_rows(h, q):
            return pl.ds((2 * h + q) * rows, rows)

        def nbr(h, axis, d):
            c = list(me[h])
            c[axis] = m4(c[axis] + d)
            return (g, tid(h, c[0], c[1]))

        def blk(h, i, d2):
            return tid(h, m4(me[h][0] + OFFS_IN[i]), m4(me[h][1] + d2))

        def msg1(h, i, k, from_buf=None):
            d2, q, d = ((2, 0, 1), (2, 1, -1), (1, 1, 1), (-1, 0, -1), (1, 0, 1), (-1, 1, -1))[k]
            s = src.at[blk(h, i, d2), q_rows(h, q)] if from_buf is None else rb.at[h, i, from_buf]
            n = h * 24 + i * 6 + k
            return rcopy(s, rb.at[h, i, k], ss.at[n], rr.at[n], nbr(h, 1, d))

        def msg2(h, k, i, from_buf=None):
            q, d = ((0, 1), (1, -1), (1, 1), (0, -1), (0, 1), (1, -1))[k]
            s = y.at[h, i, pl.ds(q * rows, rows)] if from_buf is None else rc.at[h, from_buf]
            n = 48 + h * 6 + k
            return rcopy(s, rc.at[h, k], ss.at[n], rr.at[n], nbr(h, 0, d))

        sent = []

        def go(m):
            m.start()
            sent.append(m)

        def stage_g(i):
            produce(i, blk, 0)
            for h in (0, 1):
                go(msg1(h, i, 0))
                go(msg1(h, i, 1))
            produce(i, blk, 1)
            for h in (0, 1):
                go(msg1(h, i, 2))
                go(msg1(h, i, 3))

        def stage_h(i):
            for h in (0, 1):
                msg1(h, i, 0).wait_recv()
                rb[h, i, 0] = (
                    rb[h, i, 0].astype(F32) + src[blk(h, i, 1), q_rows(h, 0)].astype(F32)
                ).astype(BF16)
                go(msg1(h, i, 4, 0))
                msg1(h, i, 1).wait_recv()
                rb[h, i, 1] = (
                    rb[h, i, 1].astype(F32) + src[blk(h, i, -1), q_rows(h, 1)].astype(F32)
                ).astype(BF16)
                go(msg1(h, i, 5, 1))

        def stage_j(i):
            produce(i, blk, 2)
            for h in (0, 1):
                for q, (k1, k2) in ((0, (3, 4)), (1, (2, 5))):
                    msg1(h, i, k1).wait_recv()
                    msg1(h, i, k2).wait_recv()
                    y[h, i, pl.ds(q * rows, rows)] = (
                        src[blk(h, i, 0), q_rows(h, q)].astype(F32)
                        + rb[h, i, k1].astype(F32)
                        + rb[h, i, k2].astype(F32)
                    ).astype(BF16)
                    if i == 0:
                        go(msg2(h, q, 0))
                if i == 1:
                    go(msg2(h, 2, 1))
                    msg2(h, 0, 1).wait_recv()
                    rc[h, 0] = (rc[h, 0].astype(F32) + y[h, 1, pl.ds(0, rows)].astype(F32)).astype(BF16)
                    go(msg2(h, 4, 1, 0))
                if i == 2:
                    go(msg2(h, 3, 2))
                    msg2(h, 1, 2).wait_recv()
                    rc[h, 1] = (rc[h, 1].astype(F32) + y[h, 2, pl.ds(rows, rows)].astype(F32)).astype(BF16)
                    go(msg2(h, 5, 2, 1))

        stage_g(0)
        stage_g(1)
        stage_h(0)
        stage_g(2)
        stage_h(1)
        stage_j(0)
        stage_g(3)
        stage_h(2)
        stage_j(1)
        stage_h(3)
        stage_j(2)
        stage_j(3)
        for h in (0, 1):
            for q, (k1, k2) in ((0, (3, 4)), (1, (2, 5))):
                msg2(h, k1, 3).wait_recv()
                msg2(h, k2, 3).wait_recv()
                finish(
                    h,
                    q,
                    y[h, 3, pl.ds(q * rows, rows)].astype(F32)
                    + rc[h, k1].astype(F32)
                    + rc[h, k2].astype(F32),
                )
        return sent

    sent1 = []

    def project(n, c):
        def third(v):
            return v + (v == 2).astype(jnp.int32)

        m = n - 7
        ox = jnp.where(n < 4, 2, jnp.where(n < 7, third(n - 4), third(m // 3)))
        oz = jnp.where(n < 4, n, jnp.where(n < 7, 2, third(lax.rem(m, 3))))
        b = m4(tz + oz) * 4 + m4(tx + ox)
        part[b] = jnp.dot(
            attn, w[:, pl.ds(pl.multiple_of(b * CW, 128), CW)], preferred_element_type=F32
        ).astype(BF16)
        return c

    def far(h, axis, o):
        c = list(me[h])
        c[axis] = m4(c[axis] + o)
        return (g, tid(h, c[0], c[1]))

    def out1(h, i, k):
        o1, o2 = OFFS_IN[i], (2, 1, -1)[k]
        n = h * 12 + i * 3 + k
        return rcopy(
            part.at[tid(h, m4(me[h][0] + o1), m4(me[h][1] + o2)), pl.ds(h * 64, 64)],
            rb1.at[h, i, k], a1s.at[n], a1r.at[n], far(h, 1, o2),
        )

    def out2(h, i):
        n = 24 + h * 3 + i
        return rcopy(y1.at[h, i], rc1.at[h, i], a1s.at[n], a1r.at[n], far(h, 0, OFFS_IN[i]))

    def go1(m):
        m.start()
        sent1.append(m)

    lax.fori_loop(0, 7, project, 0)
    for k in range(3):
        for h in (0, 1):
            go1(out1(h, 0, k))
    lax.fori_loop(7, 16, project, 0)
    for i in (1, 2, 3):
        for k in range(3):
            for h in (0, 1):
                go1(out1(h, i, k))
    small[4].wait()
    pl_m, b0, b1, sign = route_maps(routes_ref[...])
    place[...] = pl_m
    back[0] = b0
    back[1] = b1
    for c in small[5:8]:
        c.wait()
    ginv[...] = 1.0 / gain_ref[...]
    acc[...] = jnp.zeros_like(acc)
    ssq[...] = jnp.zeros_like(ssq)
    gain_row = gain_ref[:, pl.ds(pl.multiple_of(t * CW, 128), CW)]
    for i in range(4):
        for h in (0, 1):
            for k in range(3):
                out1(h, i, k).wait_recv()
            v = part[tid(h, m4(me[h][0] + OFFS_IN[i]), me[h][1]), h * 64 : h * 64 + 64, :].astype(F32)
            for k in range(3):
                v = v + rb1[h, i, k].astype(F32)
            if i < 3:
                y1[h, i] = v.astype(BF16)
                go1(out2(h, i))
            else:
                for k in range(3):
                    out2(h, k).wait_recv()
                    v = v + rc1[h, k].astype(F32)
                at = pl.ds(h * 64, 64)
                r = (res_ref[at, :].astype(F32) + v).astype(BF16)
                rs[at, :] = r
                xs[at, :] = (r.astype(F32) * gain_row).astype(BF16)

    x = xs[...]
    ds[...] = jnp.dot(place[...], x, preferred_element_type=F32).astype(BF16).reshape(8, 64, CW)

    def seat(src_y, src_c, dst_y):
        r = m4(src_y - dst_y)
        p = lax.rem(r, 2) * 2 + r // 2
        return pl.multiple_of(p * 128 + src_c * 64, 64), p * 2 + src_c

    own_row, own_slot = seat(gy, gc, gy)
    xg[t, pl.ds(own_row, 64), :] = ds[g]

    def early(c, d):
        return rcopy(
            ds.at[gy * 2 + c], xg.at[t, pl.ds(pl.multiple_of(gc * 64, 64), 64)],
            ea_s.at[c * 4 + d], ea_r.at[d * 2 + gc], (gy * 2 + c, around[d]),
        )

    def early_wait(d):
        for c in (0, 1):
            at = xg.at[around[d ^ 1], pl.ds(c * 64, 64)]
            rcopy(at, at, ea_s.at[0], ea_r.at[d * 2 + c], (g, t)).wait_recv()

    for d in range(4):
        for c in (0, 1):
            early(c, d).start()

    def deal(k):
        e = lax.rem(g + k, 8)
        row, slot = seat(gy, gc, e // 2)
        return rcopy(ds.at[e], xg.at[t, pl.ds(row, 64)], ds_s.at[k], ds_r.at[slot], (e, t))

    def deal_start(k, c):
        deal(k).start()
        return c

    lax.fori_loop(1, 8, deal_start, 0)

    def dealt(slot):
        at = xg.at[t, pl.ds(pl.multiple_of(slot * 64, 64), 64)]
        return rcopy(at, at, ds_s.at[0], ds_r.at[slot], (g, t))

    logit = lax.dot_general(
        router_ref[:, pl.ds(pl.multiple_of(t * CW, 128), CW)], x, NT, preferred_element_type=F32
    )
    diff = jnp.sum(logit * sign, axis=0, keepdims=True)
    r32 = rs[...].astype(F32)
    sq = jnp.sum(r32 * r32, axis=1, keepdims=True)
    sq = jnp.transpose(jnp.broadcast_to(sq, (128, 128)))[:8, :]
    sub8 = lax.broadcasted_iota(jnp.int32, (8, 128), 0)
    tile = jnp.where(sub8 == 0, diff, jnp.where(sub8 == 1, sq, 0.0))
    stat_out[...] = tile
    stat_in[0] = tile

    def stat(k):
        return rcopy(stat_out, stat_in.at[k], st_s.at[k], st_r.at[k], (g, lax.rem(t + k, 16)))

    def stat_start(k, c):
        stat(k).start()
        return c

    lax.fori_loop(1, 16, stat_start, 0)

    ag_sent = []

    def ag(h, phase, i, k, b):
        q, d = ((0, 1), (1, 1), (0, -1), (1, -1), (0, 1), (1, -1))[k]
        c = list(me[h])
        c[phase] = m4(c[phase] + d)
        ref = xg.at[b, pl.ds((2 * h + q) * 128, 128)]
        n = h * 30 + phase * 6 + i * 6 + k
        return rcopy(ref, ref, ags.at[n], agr.at[n], (g, tid(h, c[0], c[1])))

    def send(*a):
        m = ag(*a)
        m.start()
        ag_sent.append(m)

    def ab(h, o1, o2):
        return tid(h, m4(me[h][0] + o1), m4(me[h][1] + o2))

    def wait(h, phase, i, k, b):
        ag(h, phase, i, k, b).wait_recv()

    def spread(h, i, q):
        b = ab(h, OFFS_OUT[i], 0)
        send(h, 1, i, q, b)
        send(h, 1, i, 2 + q, b)

    def own_quarter(h, q):
        for c in (0, 1):
            dealt((2 * h + q) * 2 + c).wait_recv()
        send(h, 0, 0, q, t)
        send(h, 0, 0, 2 + q, t)

    def stage_f(i):
        for h in (0, 1):
            b = ab(h, OFFS_OUT[i], -1)
            if (i, h) == (0, 0):
                early_wait(2)
            else:
                wait(h, 1, i, 0, b)
            send(h, 1, i, 4, b)
            b = ab(h, OFFS_OUT[i], 1)
            wait(h, 1, i, 3, b)
            send(h, 1, i, 5, b)

    def stage_w1(i):
        for h in (0, 1):
            wait(h, 1, i, 1, ab(h, OFFS_OUT[i], -1))
            if (i, h) == (0, 0):
                early_wait(3)
            else:
                wait(h, 1, i, 2, ab(h, OFFS_OUT[i], 1))

    def stage_w2(i):
        for h in (0, 1):
            b = ab(h, OFFS_OUT[i], 2)
            wait(h, 1, i, 4, b)
            wait(h, 1, i, 5, b)

    def eat(*offsets):
        def body(n, c):
            h = lax.rem(n, 2)
            j = n // 2
            o1, o2 = offsets[0]
            for m, (u1, u2) in enumerate(offsets):
                o1 = jnp.where(j == m, u1, o1)
                o2 = jnp.where(j == m, u2, o2)
            c1 = m4(jnp.where(h == 0, tx, tz) + o1)
            c2 = m4(jnp.where(h == 0, tz, tx) + o2)
            b = jnp.where(h == 0, c2 * 4 + c1, c1 * 4 + c2)
            xb = xg[b, pl.ds(pl.multiple_of(h * 256, 256), 256), :]
            wat = pl.ds(pl.multiple_of(b * CW, CW), CW)
            acc[h, 0] += jnp.dot(xb, wg[wat, :], preferred_element_type=F32)
            acc[h, 1] += jnp.dot(xb, wu[wat, :], preferred_element_type=F32)
            v = xb.astype(F32) * ginv[:, pl.ds(pl.multiple_of(b * CW, 128), CW)]
            v = v * v
            ssq[h] += v[:, :128] + v[:, 128:256] + v[:, 256:]
            return c

        lax.fori_loop(0, len(offsets) * 2, body, 0)

    lo = [ab(h, -1, 0) for h in (0, 1)]
    hi = [ab(h, 1, 0) for h in (0, 1)]
    own_quarter(1, 0)
    own_quarter(1, 1)
    early_wait(0)
    send(0, 0, 0, 4, lo[0])
    spread(0, 1, 0)
    early_wait(1)
    spread(0, 2, 0)
    spread(1, 0, 0)
    spread(1, 0, 1)
    own_quarter(0, 1)
    spread(0, 0, 1)
    wait(1, 0, 0, 0, lo[1])
    send(1, 0, 0, 4, lo[1])
    wait(1, 0, 0, 3, hi[1])
    send(1, 0, 0, 5, hi[1])
    wait(0, 0, 0, 3, hi[0])
    send(0, 0, 0, 5, hi[0])
    spread(1, 1, 0)
    spread(1, 2, 1)
    spread(0, 2, 1)
    wait(0, 0, 0, 1, lo[0])
    spread(0, 1, 1)
    wait(1, 0, 0, 1, lo[1])
    spread(1, 1, 1)
    wait(1, 0, 0, 2, hi[1])
    spread(1, 2, 0)
    wcopies[0].wait()
    wcopies[1].wait()
    dealt(1 - gc).wait_recv()
    eat((0, 0))
    stage_f(0)
    for h in (0, 1):
        b = ab(h, 2, 0)
        wait(h, 0, 0, 4, b)
        spread(h, 3, 0)
        wait(h, 0, 0, 5, b)
        spread(h, 3, 1)
    eat((3, 0), (1, 0))
    stage_f(1)
    stage_w1(0)
    eat((2, 0), (0, 3), (0, 1))
    stage_f(2)
    stage_w1(1)
    eat((3, 3), (3, 1))
    stage_w2(0)
    eat((0, 2))
    stage_f(3)
    stage_w1(2)
    stage_w2(1)
    eat((1, 3), (1, 1), (3, 2))
    stage_w1(3)
    eat((2, 3), (2, 1))
    stage_w2(2)
    eat((1, 2))
    stage_w2(3)
    eat((2, 2))

    for h in (0, 1):
        total = jnp.sum(ssq[h], axis=1, keepdims=True)
        sc = lax.rsqrt(total / (16.0 * CW) + 1e-5)
        gate = acc[h, 0] * sc
        up = acc[h, 1] * sc
        hid[h] = (gate / (1.0 + jnp.exp(-gate)) * up).astype(BF16)
    wcopies[2].wait()

    def produce(i, blk, stage):
        todo = ((2,), (1, -1), (0,))[stage]
        for h in (0, 1):
            hv = hid[h]
            for d2 in todo:
                b = blk(h, i, d2)
                p2[b, h * 256 : (h + 1) * 256, :] = jnp.dot(
                    hv, wd[:, pl.ds(pl.multiple_of(b * CW, 128), CW)], preferred_element_type=F32
                ).astype(BF16)

    def back_copy(slot):
        p = slot // 2
        r = lax.rem(p, 2) * 2 + p // 2
        dst = lax.rem(gy + r, 4) * 2 + lax.rem(slot, 2)
        return rcopy(
            fin.at[pl.ds(pl.multiple_of(slot * 64, 64), 64)],
            ret.at[pl.ds(pl.multiple_of(g * 64, 64), 64)],
            rt_s.at[slot],
            rt_r.at[g],
            (dst, t),
        )

    def finish2(h, q, v):
        p = 2 * h + q
        fin[p * 128 : (p + 1) * 128, :] = v.astype(BF16)
        for c in (0, 1):
            slot = p * 2 + c
            if p == 0:

                @pl.when(gc != c)
                def _():
                    back_copy(slot).start()

                @pl.when(gc == c)
                def _():
                    ret[pl.ds(pl.multiple_of(g * 64, 64), 64), :] = fin[slot * 64 : slot * 64 + 64, :]

            else:
                back_copy(slot).start()

    sent2 = reduce_scatter(128, p2, rb2, y2, rc2, a2s, a2r, produce, finish2)

    def stat_wait(k, c):
        stat(k).wait_recv()
        return c

    lax.fori_loop(1, 16, stat_wait, 0)
    sums = jnp.sum(stat_in[...], axis=0)
    diff_all = sums[0:1, :] * lax.rsqrt(sums[1:2, :] / (16.0 * CW) + 1e-5)
    dcol = as_column(diff_all)
    wa = 1.0 / (1.0 + jnp.exp(-dcol))
    wb = 1.0 / (1.0 + jnp.exp(dcol))

    def ret_wait(k, c):
        e = lax.rem(g + k, 8)
        at = ret.at[pl.ds(pl.multiple_of(e * 64, 64), 64)]
        rcopy(at, at, rt_s.at[0], rt_r.at[e], (g, t)).wait_recv()
        return c

    lax.fori_loop(1, 8, ret_wait, 0)
    rv = ret[...]
    out_ref[...] = (
        rs[...].astype(F32)
        + wa * jnp.dot(back[0], rv, preferred_element_type=F32)
        + wb * jnp.dot(back[1], rv, preferred_element_type=F32)
    ).astype(BF16)

    for m in sent1 + ag_sent + sent2:
        m.wait_send()

    def stat_sent(k, c):
        stat(k).wait_send()
        return c

    def deal_sent(k, c):
        deal(k).wait_send()
        return c

    lax.fori_loop(1, 16, stat_sent, 0)
    lax.fori_loop(1, 8, deal_sent, 0)
    for d in range(4):
        for c in (0, 1):
            early(c, d).wait_send()
    for slot in range(8):
        if slot < 2:

            @pl.when(gc != slot)
            def _():
                back_copy(slot).wait_send()

        else:
            back_copy(slot).wait_send()


def local(
    queries, new_kv, kv_cache, page_table, context_lengths, out_weight, residual_in,
    norm_gain, router_weight, routes, gate_weight, up_weight, down_weight,
):
    pool = kv_cache.shape[0] * kv_cache.shape[2]
    hb = pl.BlockSpec(memory_space=pl.ANY)
    dma = pltpu.SemaphoreType.DMA
    return pl.pallas_call(
        layer_kernel,
        out_shape=jax.ShapeDtypeStruct((128, CW), BF16),
        in_specs=[hb] * 13,
        out_specs=pl.BlockSpec(memory_space=pltpu.VMEM),
        scratch_shapes=[
            pltpu.VMEM((128, 256), BF16),
            pltpu.VMEM((128, 256), BF16),
            pltpu.VMEM((16, 128), jnp.int32),
            pltpu.VMEM((1, 128), jnp.int32),
            pltpu.VMEM((pool, 256), BF16),
            pltpu.VMEM((256, 16 * CW), BF16),
            pltpu.VMEM((128, CW), BF16),
            pltpu.VMEM((1, 16 * CW), F32),
            pltpu.VMEM((8, 16 * CW), BF16),
            pltpu.VMEM((2, 128), jnp.int32),
            pltpu.VMEM((pool // 16, 128), BF16),
            pltpu.VMEM((16, 128, CW), BF16),
            pltpu.VMEM((1, 16 * CW), F32),
            pltpu.VMEM((16 * CW, FW), BF16),
            pltpu.VMEM((16 * CW, FW), BF16),
            pltpu.VMEM((FW, 16 * CW), BF16),
            pltpu.VMEM((16, 512, CW), BF16),
            pltpu.VMEM((2, 2, 256, FW), F32),
            pltpu.VMEM((2, 256, 128), F32),
            pltpu.VMEM((2, 256, FW), BF16),
            pltpu.VMEM((16, 512, CW), BF16),
            pltpu.VMEM((2, 4, 3, 64, CW), BF16),
            pltpu.VMEM((2, 3, 64, CW), BF16),
            pltpu.VMEM((2, 3, 64, CW), BF16),
            pltpu.VMEM((2, 4, 6, 128, CW), BF16),
            pltpu.VMEM((2, 4, 256, CW), BF16),
            pltpu.VMEM((2, 6, 128, CW), BF16),
            pltpu.VMEM((128, CW), BF16),
            pltpu.VMEM((128, CW), BF16),
            pltpu.VMEM((8, 64, CW), BF16),
            pltpu.VMEM((512, CW), BF16),
            pltpu.VMEM((512, CW), BF16),
            pltpu.VMEM((8, 128), F32),
            pltpu.VMEM((16, 8, 128), F32),
            pltpu.VMEM((512, 128), BF16),
            pltpu.VMEM((2, 128, 512), BF16),
            dma((PARTS,)),
            dma((9,)),
            dma((3,)),
            dma((30,)),
            dma((30,)),
            dma((60,)),
            dma((60,)),
            dma((60,)),
            dma((60,)),
            dma((8,)),
            dma((8,)),
            dma((8,)),
            dma((8,)),
            dma((8,)),
            dma((8,)),
            dma((16,)),
            dma((16,)),
        ],
        compiler_params=pltpu.CompilerParams(
            collective_id=0, has_side_effects=True, vmem_limit_bytes=60 * 1024 * 1024
        ),
        cost_estimate=pl.CostEstimate(flops=11 << 30, bytes_accessed=26 << 20, transcendentals=1 << 21),
        name="layer",
    )(
        queries,
        new_kv.reshape(128, 256),
        page_table.T,
        context_lengths.reshape(1, 128),
        kv_cache.reshape(pool, 256),
        out_weight,
        residual_in,
        norm_gain.reshape(1, 16 * CW),
        router_weight.T,
        routes.T,
        gate_weight,
        up_weight,
        down_weight,
    )


def solution(mesh):
    return jax.shard_map(
        local,
        mesh=mesh,
        in_specs=(
            P("grp", "tp"),
            P("grp", "tp", None),
            P("grp", "tp", None, None),
            P("grp", None),
            P("grp"),
            P("tp", None),
            P("grp", "tp"),
            P(),
            P(),
            P("grp", None),
            P("grp", None, "tp"),
            P("grp", None, "tp"),
            P("grp", "tp", None),
        ),
        out_specs=P("grp", "tp"),
        check_vma=False,
    )
```

```python
import jax
import jax.numpy as jnp
from jax import lax
from jax.experimental import pallas as pl
from jax.experimental.pallas import tpu as pltpu
from jax.sharding import PartitionSpec as P

F32 = jnp.float32
BF16 = jnp.bfloat16
MESH = pl.DeviceIdType.MESH
NT = (((1,), (1,)), ((), ()))
TN = (((0,), (0,)), ((), ()))
PARTS = 5
NEG = -1e30
CW = 384
FW = 512
OFFS_OUT = (0, 3, 1, 2)
OFFS_IN = (2, 1, 3, 0)


def attend(q, own, live_ref, kv, kv_copies, part_rows):
    q2 = jnp.concatenate([q[:, :128], q[:, 128:]], axis=0)
    pages = part_rows // 16
    tok = lax.broadcasted_iota(jnp.int32, (256, 128), 0)
    offs = (tok & 15).astype(F32)
    tok16 = lax.broadcasted_iota(jnp.int32, (256, 16), 0) >> 4
    spread = (tok16 == lax.broadcasted_iota(jnp.int32, (256, 16), 1)).astype(F32).astype(BF16)
    s_own = lax.dot_general(own[:, :128], q2, NT, preferred_element_type=F32)
    row = lax.broadcasted_iota(jnp.int32, (128, 128), 0)
    col = lax.broadcasted_iota(jnp.int32, (128, 128), 1)
    eye = (row == col).astype(F32)
    eye = jnp.concatenate([eye, eye], axis=1)
    top = jnp.sum(s_own * eye, axis=0, keepdims=True)
    tot = jnp.ones((8, 256), F32) * 0.125
    own_v = jnp.transpose(own[:, 128:].astype(F32))
    acc = jnp.concatenate([own_v, own_v], axis=1)
    scale = 128.0 ** -0.5
    for i, copy in enumerate(kv_copies):
        copy.wait()
        tiles = []
        peak = top
        for c in range(part_rows // 256):
            at = i * part_rows + c * 256
            s = lax.dot_general(kv[at : at + 256, :128], q2, NT, preferred_element_type=F32)
            cn = live_ref[i * pages + c * 16 : i * pages + c * 16 + 16, :]
            m = offs < jnp.dot(spread, cn, preferred_element_type=F32)
            s = jnp.concatenate([jnp.where(m, s[:, :128], NEG), jnp.where(m, s[:, 128:], NEG)], axis=1)
            tiles.append(s)
            peak = jnp.maximum(peak, jnp.max(jnp.max(s.reshape(32, 8, 256), axis=0), axis=0, keepdims=True))
        fade = jnp.exp((top - peak) * scale)
        top = peak
        tot = tot * fade
        ps = []
        for s in tiles:
            p = jnp.exp((s - top) * scale)
            tot = tot + jnp.sum(p.reshape(32, 8, 256), axis=0)
            ps.append(p.astype(BF16))
        p = jnp.concatenate(ps, axis=0)
        acc = acc * fade + lax.dot_general(
            kv[i * part_rows : (i + 1) * part_rows, 128:], p, TN, preferred_element_type=F32
        )
    att = acc / jnp.sum(tot, axis=0, keepdims=True)
    return jnp.concatenate([jnp.transpose(att[:, :128]), jnp.transpose(att[:, 128:])], axis=1).astype(BF16)


def as_column(row):
    return jnp.transpose(jnp.broadcast_to(row, (128, 128)))[:, 0:1]


def route_maps(routes):
    lane = lax.broadcasted_iota(jnp.int32, (128, 128), 1)
    sub = lax.broadcasted_iota(jnp.int32, (128, 128), 0)
    hit0 = (sub == routes[0:1, :]).astype(F32)
    hit1 = (sub == routes[1:2, :]).astype(F32)
    hit = hit0 + hit1
    rank = jnp.dot(hit.astype(BF16), (sub < lane).astype(F32).astype(BF16), preferred_element_type=F32)
    spot = jnp.where(hit > 0.5, rank, -1.0)
    slot = lax.broadcasted_iota(jnp.int32, (64, 128), 0).astype(F32)
    place = jnp.concatenate([(slot == spot[e : e + 1, :]).astype(F32) for e in range(8)], axis=0)
    wide = lax.broadcasted_iota(jnp.int32, (128, 512), 1).astype(F32)

    def back(h, r):
        at = r.astype(F32) * 64.0 + jnp.sum(h * rank, axis=0, keepdims=True)
        return (wide == as_column(at)).astype(F32).astype(BF16)

    sign = hit0[:8, :] - hit1[:8, :]
    return place.astype(BF16), back(hit0, routes[0:1, :]), back(hit1, routes[1:2, :]), sign


def layer_kernel(
    q_hbm, own_hbm, pt_hbm, len_hbm, kv_hbm, w_hbm, res_hbm, gain_hbm, router_hbm, routes_hbm, wg_hbm, wu_hbm, wd_hbm,
    out_ref,
    q_ref, own_ref, pt_ref, len_ref, kv, w, res_ref, gain_ref, router_ref, routes_ref, live, part, ginv,
    wg, wu, wd, xg, acc, ssq, hid, p2, rb1, y1, rc1, rb2, y2, rc2,
    rs, xs, ds, fin, ret, stat_out, stat_in, place, back,
    ksem, msem, wsem, a1s, a1r, ags, agr, a2s, a2r, ds_s, ds_r, ea_s, ea_r, rt_s, rt_r, st_s, st_r,
):
    g = lax.axis_index("grp")
    t = lax.axis_index("tp")
    gy, gc = g // 2, lax.rem(g, 2)
    tz, tx = t // 4, lax.rem(t, 4)
    me = ((tx, tz), (tz, tx))

    def tid(h, c1, c2):
        return c2 * 4 + c1 if h == 0 else c1 * 4 + c2

    def m4(v):
        return lax.rem(v + 4, 4)

    barrier = pltpu.get_barrier_semaphore()

    def greet_t(k, c):
        pl.semaphore_signal(barrier, inc=1, device_id=(g, lax.rem(t + k, 16)), device_id_type=MESH)
        return c

    def greet_g(k, c):
        pl.semaphore_signal(barrier, inc=1, device_id=(lax.rem(g + k, 8), t), device_id_type=MESH)
        return c

    around = (
        tz * 4 + m4(tx + 1), tz * 4 + m4(tx - 1), m4(tz + 1) * 4 + tx, m4(tz - 1) * 4 + tx,
    )
    for a in around:
        pl.semaphore_signal(barrier, inc=1, device_id=(gy * 2 + 1 - gc, a), device_id_type=MESH)
    lax.fori_loop(1, 16, greet_t, 0)
    lax.fori_loop(1, 8, greet_g, 0)

    step = kv.shape[0] // PARTS
    small = [
        pltpu.make_async_copy(src, dst, msem.at[i])
        for i, (src, dst) in enumerate(
            (
                (pt_hbm, pt_ref), (len_hbm, len_ref), (q_hbm, q_ref), (own_hbm, own_ref), (routes_hbm, routes_ref),
                (res_hbm, res_ref), (gain_hbm, gain_ref), (router_hbm, router_ref), (w_hbm, w),
            )
        )
    ]
    kv_copies = [
        pltpu.make_async_copy(kv_hbm.at[pl.ds(i * step, step)], kv.at[pl.ds(i * step, step)], ksem.at[i])
        for i in range(PARTS)
    ]
    wcopies = [
        pltpu.make_async_copy(src.at[0], dst, wsem.at[i])
        for i, (src, dst) in enumerate(((wg_hbm, wg), (wu_hbm, wu), (wd_hbm, wd)))
    ]
    for c in small[:5] + kv_copies + small[5:] + wcopies:
        c.start()

    small[0].wait()
    small[1].wait()
    pages = live.shape[0]
    page_ids = lax.broadcasted_iota(jnp.int32, (pages, 128), 0)
    lens = len_ref[...]
    count = jnp.zeros((pages, 128), jnp.int32)
    for j in range(16):
        here = jnp.clip(lens - 16 * j, 0, 16)
        count = count + jnp.where(page_ids == pt_ref[j : j + 1, :], here, 0)
    live[...] = count.astype(F32).astype(BF16)
    small[2].wait()
    small[3].wait()
    attn = attend(q_ref[...], own_ref[...], live, kv, kv_copies, step)
    small[8].wait()

    pl.semaphore_wait(barrier, 26)

    def rcopy(src, dst, ss, rr, dev):
        return pltpu.make_async_remote_copy(
            src_ref=src, dst_ref=dst, send_sem=ss, recv_sem=rr, device_id=dev, device_id_type=MESH
        )

    def reduce_scatter(rows, src, rb, y, rc, ss, rr, produce, finish):
        def q_rows(h, q):
            return pl.ds((2 * h + q) * rows, rows)

        def nbr(h, axis, d):
            c = list(me[h])
            c[axis] = m4(c[axis] + d)
            return (g, tid(h, c[0], c[1]))

        def blk(h, i, d2):
            return tid(h, m4(me[h][0] + OFFS_IN[i]), m4(me[h][1] + d2))

        def msg1(h, i, k, from_buf=None):
            d2, q, d = ((2, 0, 1), (2, 1, -1), (1, 1, 1), (-1, 0, -1), (1, 0, 1), (-1, 1, -1))[k]
            s = src.at[blk(h, i, d2), q_rows(h, q)] if from_buf is None else rb.at[h, i, from_buf]
            n = h * 24 + i * 6 + k
            return rcopy(s, rb.at[h, i, k], ss.at[n], rr.at[n], nbr(h, 1, d))

        def msg2(h, k, i, from_buf=None):
            q, d = ((0, 1), (1, -1), (1, 1), (0, -1), (0, 1), (1, -1))[k]
            s = y.at[h, i, pl.ds(q * rows, rows)] if from_buf is None else rc.at[h, from_buf]
            n = 48 + h * 6 + k
            return rcopy(s, rc.at[h, k], ss.at[n], rr.at[n], nbr(h, 0, d))

        sent = []

        def go(m):
            m.start()
            sent.append(m)

        def stage_g(i):
            produce(i, blk, 0)
            for h in (0, 1):
                go(msg1(h, i, 0))
                go(msg1(h, i, 1))
            produce(i, blk, 1)
            for h in (0, 1):
                go(msg1(h, i, 2))
                go(msg1(h, i, 3))

        def stage_h(i):
            for h in (0, 1):
                msg1(h, i, 0).wait_recv()
                rb[h, i, 0] = (
                    rb[h, i, 0].astype(F32) + src[blk(h, i, 1), q_rows(h, 0)].astype(F32)
                ).astype(BF16)
                go(msg1(h, i, 4, 0))
                msg1(h, i, 1).wait_recv()
                rb[h, i, 1] = (
                    rb[h, i, 1].astype(F32) + src[blk(h, i, -1), q_rows(h, 1)].astype(F32)
                ).astype(BF16)
                go(msg1(h, i, 5, 1))

        def stage_j(i):
            produce(i, blk, 2)
            for h in (0, 1):
                for q, (k1, k2) in ((0, (3, 4)), (1, (2, 5))):
                    msg1(h, i, k1).wait_recv()
                    msg1(h, i, k2).wait_recv()
                    y[h, i, pl.ds(q * rows, rows)] = (
                        src[blk(h, i, 0), q_rows(h, q)].astype(F32)
                        + rb[h, i, k1].astype(F32)
                        + rb[h, i, k2].astype(F32)
                    ).astype(BF16)
                    if i == 0:
                        go(msg2(h, q, 0))
                if i == 1:
                    go(msg2(h, 2, 1))
                    msg2(h, 0, 1).wait_recv()
                    rc[h, 0] = (rc[h, 0].astype(F32) + y[h, 1, pl.ds(0, rows)].astype(F32)).astype(BF16)
                    go(msg2(h, 4, 1, 0))
                if i == 2:
                    go(msg2(h, 3, 2))
                    msg2(h, 1, 2).wait_recv()
                    rc[h, 1] = (rc[h, 1].astype(F32) + y[h, 2, pl.ds(rows, rows)].astype(F32)).astype(BF16)
                    go(msg2(h, 5, 2, 1))

        stage_g(0)
        stage_g(1)
        stage_h(0)
        stage_g(2)
        stage_h(1)
        stage_j(0)
        stage_g(3)
        stage_h(2)
        stage_j(1)
        stage_h(3)
        stage_j(2)
        stage_j(3)
        for h in (0, 1):
            for q, (k1, k2) in ((0, (3, 4)), (1, (2, 5))):
                msg2(h, k1, 3).wait_recv()
                msg2(h, k2, 3).wait_recv()
                finish(
                    h,
                    q,
                    y[h, 3, pl.ds(q * rows, rows)].astype(F32)
                    + rc[h, k1].astype(F32)
                    + rc[h, k2].astype(F32),
                )
        return sent

    sent1 = []

    def project(n, c):
        def third(v):
            return v + (v == 2).astype(jnp.int32)

        m = n - 7
        ox = jnp.where(n < 4, 2, jnp.where(n < 7, third(n - 4), third(m // 3)))
        oz = jnp.where(n < 4, n, jnp.where(n < 7, 2, third(lax.rem(m, 3))))
        b = m4(tz + oz) * 4 + m4(tx + ox)
        part[b] = jnp.dot(
            attn, w[:, pl.ds(pl.multiple_of(b * CW, 128), CW)], preferred_element_type=F32
        ).astype(BF16)
        return c

    def far(h, axis, o):
        c = list(me[h])
        c[axis] = m4(c[axis] + o)
        return (g, tid(h, c[0], c[1]))

    def cols(kc):
        return pl.ds(kc * 128, 128)

    def out1(h, i, k, kc):
        o1, o2 = OFFS_IN[i], (2, 1, -1)[k]
        n = kc * 30 + h * 12 + i * 3 + k
        return rcopy(
            part.at[tid(h, m4(me[h][0] + o1), m4(me[h][1] + o2)), pl.ds(h * 64, 64), cols(kc)],
            rb1.at[h, i, k, :, cols(kc)], a1s.at[n], a1r.at[n], far(h, 1, o2),
        )

    def out2(h, i, kc):
        n = kc * 30 + 24 + h * 3 + i
        return rcopy(
            y1.at[h, i, :, cols(kc)], rc1.at[h, i, :, cols(kc)], a1s.at[n], a1r.at[n], far(h, 0, OFFS_IN[i])
        )

    def go1(m):
        m.start()
        sent1.append(m)

    def first_step(kc, groups):
        for i in groups:
            for k in range(3):
                for h in (0, 1):
                    go1(out1(h, i, k, kc))

    def term1(h, i, kc):
        for k in range(3):
            out1(h, i, k, kc).wait_recv()
        v = part[tid(h, m4(me[h][0] + OFFS_IN[i]), me[h][1]), h * 64 : h * 64 + 64, cols(kc)].astype(F32)
        for k in range(3):
            v = v + rb1[h, i, k, :, cols(kc)].astype(F32)
        return v

    def second_step(kc):
        for i in range(3):
            for h in (0, 1):
                y1[h, i, :, cols(kc)] = term1(h, i, kc).astype(BF16)
                go1(out2(h, i, kc))

    def finish1(kc):
        gain_row = gain_ref[:, pl.ds(pl.multiple_of(t * CW + kc * 128, 128), 128)]
        for h in (0, 1):
            v = term1(h, 3, kc)
            for k in range(3):
                out2(h, k, kc).wait_recv()
                v = v + rc1[h, k, :, cols(kc)].astype(F32)
            at = pl.ds(h * 64, 64)
            r = (res_ref[at, cols(kc)].astype(F32) + v).astype(BF16)
            rs[at, cols(kc)] = r
            xs[at, cols(kc)] = (r.astype(F32) * gain_row).astype(BF16)

    def seat(src_y, src_c, dst_y):
        r = m4(src_y - dst_y)
        p = lax.rem(r, 2) * 2 + r // 2
        return pl.multiple_of(p * 128 + src_c * 64, 64), p * 2 + src_c

    own_row, own_slot = seat(gy, gc, gy)

    def early(c, d, kc):
        return rcopy(
            ds.at[gy * 2 + c, :, cols(kc)], xg.at[t, pl.ds(pl.multiple_of(gc * 64, 64), 64), cols(kc)],
            ea_s.at[kc * 8 + c * 4 + d], ea_r.at[kc * 8 + d * 2 + gc], (gy * 2 + c, around[d]),
        )

    def early_wait(d):
        for c in (0, 1):
            for kc in range(3):
                at = xg.at[around[d ^ 1], pl.ds(c * 64, 64), cols(kc)]
                rcopy(at, at, ea_s.at[0], ea_r.at[kc * 8 + d * 2 + c], (g, t)).wait_recv()

    def deal(k, kc):
        e = lax.rem(g + k, 8)
        row, slot = seat(gy, gc, e // 2)
        return rcopy(
            ds.at[e, :, cols(kc)], xg.at[t, pl.ds(row, 64), cols(kc)],
            ds_s.at[kc * 8 + k], ds_r.at[kc * 8 + slot], (e, t),
        )

    def dealt(slot, kc):
        at = xg.at[t, pl.ds(pl.multiple_of(slot * 64, 64), 64), cols(kc)]
        return rcopy(at, at, ds_s.at[0], ds_r.at[kc * 8 + slot], (g, t))

    def deal_out(kc):
        ds[:, :, cols(kc)] = (
            jnp.dot(place[...], xs[:, cols(kc)], preferred_element_type=F32).astype(BF16).reshape(8, 64, 128)
        )
        xg[t, pl.ds(own_row, 64), cols(kc)] = ds[g, :, cols(kc)]
        for d in range(4):
            for c in (0, 1):
                early(c, d, kc).start()

        def deal_start(k, c):
            deal(k, kc).start()
            return c

        lax.fori_loop(1, 8, deal_start, 0)

    ag_sent = []

    def ag(h, phase, i, k, b, kc=None):
        q, d = ((0, 1), (1, 1), (0, -1), (1, -1), (0, 1), (1, -1))[k]
        c = list(me[h])
        c[phase] = m4(c[phase] + d)
        rows = pl.ds((2 * h + q) * 128, 128)
        ref = xg.at[b, rows] if kc is None else xg.at[b, rows, cols(kc)]
        n = h * 30 + phase * 6 + i * 6 + k + (0 if kc is None else 60 * kc)
        return rcopy(ref, ref, ags.at[n], agr.at[n], (g, tid(h, c[0], c[1])))

    def send(*a):
        m = ag(*a)
        m.start()
        ag_sent.append(m)

    def ab(h, o1, o2):
        return tid(h, m4(me[h][0] + o1), m4(me[h][1] + o2))

    def wait(h, phase, i, k, b):
        if k < 4 and i == 0:
            for kc in range(3):
                ag(h, phase, i, k, b, kc).wait_recv()
        else:
            ag(h, phase, i, k, b).wait_recv()

    def spread(h, i, q):
        b = ab(h, OFFS_OUT[i], 0)
        send(h, 1, i, q, b)
        send(h, 1, i, 2 + q, b)

    def own_sends(kc):
        for h, q in ((1, 0), (1, 1), (0, 1)):
            for c in (0, 1):
                dealt((2 * h + q) * 2 + c, kc).wait_recv()
            for phase in (0, 1):
                for k in (q, 2 + q):
                    send(h, phase, 0, k, t, kc)

    lax.fori_loop(0, 7, project, 0)
    first_step(0, (0,))
    lax.fori_loop(7, 16, project, 0)
    first_step(0, (1, 2, 3))
    first_step(1, (0, 1, 2, 3))
    small[4].wait()
    pl_m, b0, b1, sign = route_maps(routes_ref[...])
    place[...] = pl_m
    back[0] = b0
    back[1] = b1
    for c in small[5:8]:
        c.wait()
    second_step(0)
    first_step(2, (0, 1, 2, 3))
    second_step(1)
    finish1(0)
    deal_out(0)
    second_step(2)
    finish1(1)
    deal_out(1)
    own_sends(0)
    finish1(2)
    deal_out(2)
    own_sends(1)
    x = xs[...]

    logit = lax.dot_general(
        router_ref[:, pl.ds(pl.multiple_of(t * CW, 128), CW)], x, NT, preferred_element_type=F32
    )
    diff = jnp.sum(logit * sign, axis=0, keepdims=True)
    r32 = rs[...].astype(F32)
    sq = jnp.sum(r32 * r32, axis=1, keepdims=True)
    sq = jnp.transpose(jnp.broadcast_to(sq, (128, 128)))[:8, :]
    sub8 = lax.broadcasted_iota(jnp.int32, (8, 128), 0)
    tile = jnp.where(sub8 == 0, diff, jnp.where(sub8 == 1, sq, 0.0))
    stat_out[...] = tile
    stat_in[0] = tile

    def stat(k):
        return rcopy(stat_out, stat_in.at[k], st_s.at[k], st_r.at[k], (g, lax.rem(t + k, 16)))

    def stat_start(k, c):
        stat(k).start()
        return c

    lax.fori_loop(1, 16, stat_start, 0)

    def stage_f(i):
        for h in (0, 1):
            b = ab(h, OFFS_OUT[i], -1)
            if (i, h) == (0, 0):
                early_wait(2)
            else:
                wait(h, 1, i, 0, b)
            send(h, 1, i, 4, b)
            b = ab(h, OFFS_OUT[i], 1)
            wait(h, 1, i, 3, b)
            send(h, 1, i, 5, b)

    def stage_w1(i):
        for h in (0, 1):
            wait(h, 1, i, 1, ab(h, OFFS_OUT[i], -1))
            if (i, h) == (0, 0):
                early_wait(3)
            else:
                wait(h, 1, i, 2, ab(h, OFFS_OUT[i], 1))

    def stage_w2(i):
        for h in (0, 1):
            b = ab(h, OFFS_OUT[i], 2)
            wait(h, 1, i, 4, b)
            wait(h, 1, i, 5, b)

    def eat(*offsets):
        def body(n, c):
            h = lax.rem(n, 2)
            j = n // 2
            o1, o2 = offsets[0]
            for m, (u1, u2) in enumerate(offsets):
                o1 = jnp.where(j == m, u1, o1)
                o2 = jnp.where(j == m, u2, o2)
            c1 = m4(jnp.where(h == 0, tx, tz) + o1)
            c2 = m4(jnp.where(h == 0, tz, tx) + o2)
            b = jnp.where(h == 0, c2 * 4 + c1, c1 * 4 + c2)
            xb = xg[b, pl.ds(pl.multiple_of(h * 256, 256), 256), :]
            wat = pl.ds(pl.multiple_of(b * CW, CW), CW)
            acc[h, 0] += jnp.dot(xb, wg[wat, :], preferred_element_type=F32)
            acc[h, 1] += jnp.dot(xb, wu[wat, :], preferred_element_type=F32)
            v = xb.astype(F32) * ginv[:, pl.ds(pl.multiple_of(b * CW, 128), CW)]
            v = v * v
            ssq[h] += v[:, :128] + v[:, 128:256] + v[:, 256:]
            return c

        lax.fori_loop(0, len(offsets) * 2, body, 0)

    lo = [ab(h, -1, 0) for h in (0, 1)]
    hi = [ab(h, 1, 0) for h in (0, 1)]
    own_sends(2)
    ginv[...] = 1.0 / gain_ref[...]
    acc[...] = jnp.zeros_like(acc)
    ssq[...] = jnp.zeros_like(ssq)
    early_wait(0)
    send(0, 0, 0, 4, lo[0])
    spread(0, 1, 0)
    early_wait(1)
    spread(0, 2, 0)
    wait(1, 0, 0, 0, lo[1])
    send(1, 0, 0, 4, lo[1])
    wait(1, 0, 0, 3, hi[1])
    send(1, 0, 0, 5, hi[1])
    wait(0, 0, 0, 3, hi[0])
    send(0, 0, 0, 5, hi[0])
    spread(1, 1, 0)
    spread(1, 2, 1)
    spread(0, 2, 1)
    wait(0, 0, 0, 1, lo[0])
    spread(0, 1, 1)
    wait(1, 0, 0, 1, lo[1])
    spread(1, 1, 1)
    wait(1, 0, 0, 2, hi[1])
    spread(1, 2, 0)
    wcopies[0].wait()
    wcopies[1].wait()
    for kc in range(3):
        dealt(1 - gc, kc).wait_recv()
    eat((0, 0))
    stage_f(0)
    for h in (0, 1):
        b = ab(h, 2, 0)
        wait(h, 0, 0, 4, b)
        spread(h, 3, 0)
        wait(h, 0, 0, 5, b)
        spread(h, 3, 1)
    eat((3, 0), (1, 0))
    stage_f(1)
    stage_w1(0)
    eat((2, 0), (0, 3), (0, 1))
    stage_f(2)
    stage_w1(1)
    eat((3, 3), (3, 1))
    stage_w2(0)
    eat((0, 2))
    stage_f(3)
    stage_w1(2)
    stage_w2(1)
    eat((1, 3), (1, 1), (3, 2))
    stage_w1(3)
    eat((2, 3), (2, 1))
    stage_w2(2)
    eat((1, 2))
    stage_w2(3)
    eat((2, 2))

    for h in (0, 1):
        total = jnp.sum(ssq[h], axis=1, keepdims=True)
        sc = lax.rsqrt(total / (16.0 * CW) + 1e-5)
        gate = acc[h, 0] * sc
        up = acc[h, 1] * sc
        hid[h] = (gate / (1.0 + jnp.exp(-gate)) * up).astype(BF16)
    wcopies[2].wait()

    def produce(i, blk, stage):
        todo = ((2,), (1, -1), (0,))[stage]
        for h in (0, 1):
            hv = hid[h]
            for d2 in todo:
                b = blk(h, i, d2)
                p2[b, h * 256 : (h + 1) * 256, :] = jnp.dot(
                    hv, wd[:, pl.ds(pl.multiple_of(b * CW, 128), CW)], preferred_element_type=F32
                ).astype(BF16)

    def back_copy(slot):
        p = slot // 2
        r = lax.rem(p, 2) * 2 + p // 2
        dst = lax.rem(gy + r, 4) * 2 + lax.rem(slot, 2)
        return rcopy(
            fin.at[pl.ds(pl.multiple_of(slot * 64, 64), 64)],
            ret.at[pl.ds(pl.multiple_of(g * 64, 64), 64)],
            rt_s.at[slot],
            rt_r.at[g],
            (dst, t),
        )

    def finish2(h, q, v):
        p = 2 * h + q
        fin[p * 128 : (p + 1) * 128, :] = v.astype(BF16)
        for c in (0, 1):
            slot = p * 2 + c
            if p == 0:

                @pl.when(gc != c)
                def _():
                    back_copy(slot).start()

                @pl.when(gc == c)
                def _():
                    ret[pl.ds(pl.multiple_of(g * 64, 64), 64), :] = fin[slot * 64 : slot * 64 + 64, :]

            else:
                back_copy(slot).start()

    sent2 = reduce_scatter(128, p2, rb2, y2, rc2, a2s, a2r, produce, finish2)

    def stat_wait(k, c):
        stat(k).wait_recv()
        return c

    lax.fori_loop(1, 16, stat_wait, 0)
    sums = jnp.sum(stat_in[...], axis=0)
    diff_all = sums[0:1, :] * lax.rsqrt(sums[1:2, :] / (16.0 * CW) + 1e-5)
    dcol = as_column(diff_all)
    wa = 1.0 / (1.0 + jnp.exp(-dcol))
    wb = 1.0 / (1.0 + jnp.exp(dcol))

    def ret_wait(k, c):
        e = lax.rem(g + k, 8)
        at = ret.at[pl.ds(pl.multiple_of(e * 64, 64), 64)]
        rcopy(at, at, rt_s.at[0], rt_r.at[e], (g, t)).wait_recv()
        return c

    lax.fori_loop(1, 8, ret_wait, 0)
    rv = ret[...]
    out_ref[...] = (
        rs[...].astype(F32)
        + wa * jnp.dot(back[0], rv, preferred_element_type=F32)
        + wb * jnp.dot(back[1], rv, preferred_element_type=F32)
    ).astype(BF16)

    for m in sent1 + ag_sent + sent2:
        m.wait_send()

    def stat_sent(k, c):
        stat(k).wait_send()
        return c

    def deal_sent(k, c):
        for kc in range(3):
            deal(k, kc).wait_send()
        return c

    lax.fori_loop(1, 16, stat_sent, 0)
    lax.fori_loop(1, 8, deal_sent, 0)
    for d in range(4):
        for c in (0, 1):
            for kc in range(3):
                early(c, d, kc).wait_send()
    for slot in range(8):
        if slot < 2:

            @pl.when(gc != slot)
            def _():
                back_copy(slot).wait_send()

        else:
            back_copy(slot).wait_send()


def local(
    queries, new_kv, kv_cache, page_table, context_lengths, out_weight, residual_in,
    norm_gain, router_weight, routes, gate_weight, up_weight, down_weight,
):
    pool = kv_cache.shape[0] * kv_cache.shape[2]
    hb = pl.BlockSpec(memory_space=pl.ANY)
    dma = pltpu.SemaphoreType.DMA
    return pl.pallas_call(
        layer_kernel,
        out_shape=jax.ShapeDtypeStruct((128, CW), BF16),
        in_specs=[hb] * 13,
        out_specs=pl.BlockSpec(memory_space=pltpu.VMEM),
        scratch_shapes=[
            pltpu.VMEM((128, 256), BF16),
            pltpu.VMEM((128, 256), BF16),
            pltpu.VMEM((16, 128), jnp.int32),
            pltpu.VMEM((1, 128), jnp.int32),
            pltpu.VMEM((pool, 256), BF16),
            pltpu.VMEM((256, 16 * CW), BF16),
            pltpu.VMEM((128, CW), BF16),
            pltpu.VMEM((1, 16 * CW), F32),
            pltpu.VMEM((8, 16 * CW), BF16),
            pltpu.VMEM((2, 128), jnp.int32),
            pltpu.VMEM((pool // 16, 128), BF16),
            pltpu.VMEM((16, 128, CW), BF16),
            pltpu.VMEM((1, 16 * CW), F32),
            pltpu.VMEM((16 * CW, FW), BF16),
            pltpu.VMEM((16 * CW, FW), BF16),
            pltpu.VMEM((FW, 16 * CW), BF16),
            pltpu.VMEM((16, 512, CW), BF16),
            pltpu.VMEM((2, 2, 256, FW), F32),
            pltpu.VMEM((2, 256, 128), F32),
            pltpu.VMEM((2, 256, FW), BF16),
            pltpu.VMEM((16, 512, CW), BF16),
            pltpu.VMEM((2, 4, 3, 64, CW), BF16),
            pltpu.VMEM((2, 3, 64, CW), BF16),
            pltpu.VMEM((2, 3, 64, CW), BF16),
            pltpu.VMEM((2, 4, 6, 128, CW), BF16),
            pltpu.VMEM((2, 4, 256, CW), BF16),
            pltpu.VMEM((2, 6, 128, CW), BF16),
            pltpu.VMEM((128, CW), BF16),
            pltpu.VMEM((128, CW), BF16),
            pltpu.VMEM((8, 64, CW), BF16),
            pltpu.VMEM((512, CW), BF16),
            pltpu.VMEM((512, CW), BF16),
            pltpu.VMEM((8, 128), F32),
            pltpu.VMEM((16, 8, 128), F32),
            pltpu.VMEM((512, 128), BF16),
            pltpu.VMEM((2, 128, 512), BF16),
            dma((PARTS,)),
            dma((9,)),
            dma((3,)),
            dma((90,)),
            dma((90,)),
            dma((180,)),
            dma((180,)),
            dma((60,)),
            dma((60,)),
            dma((24,)),
            dma((24,)),
            dma((24,)),
            dma((24,)),
            dma((8,)),
            dma((8,)),
            dma((16,)),
            dma((16,)),
        ],
        compiler_params=pltpu.CompilerParams(
            collective_id=0, has_side_effects=True, vmem_limit_bytes=60 * 1024 * 1024
        ),
        cost_estimate=pl.CostEstimate(flops=11 << 30, bytes_accessed=26 << 20, transcendentals=1 << 21),
        name="layer",
    )(
        queries,
        new_kv.reshape(128, 256),
        page_table.T,
        context_lengths.reshape(1, 128),
        kv_cache.reshape(pool, 256),
        out_weight,
        residual_in,
        norm_gain.reshape(1, 16 * CW),
        router_weight.T,
        routes.T,
        gate_weight,
        up_weight,
        down_weight,
    )


def solution(mesh):
    return jax.shard_map(
        local,
        mesh=mesh,
        in_specs=(
            P("grp", "tp"),
            P("grp", "tp", None),
            P("grp", "tp", None, None),
            P("grp", None),
            P("grp"),
            P("tp", None),
            P("grp", "tp"),
            P(),
            P(),
            P("grp", None),
            P("grp", None, "tp"),
            P("grp", None, "tp"),
            P("grp", "tp", None),
        ),
        out_specs=P("grp", "tp"),
        check_vma=False,
    )
```
